32 devices in a mesh: dp: 16 (over z, x, core), tensor: 2 (over y).
Axes of the slice: x: 2, y: 2, z: 4, core: 2. Of those that a mesh axis runs over, the one named last changes fastest.
Arguments:
- frames: bfloat16 [2, 16384, 1280], P(None, ('dp', 'tensor')), may hold values from -6 to 6
- cotangent: bfloat16 [2, 16384, 1280], P(None, ('dp', 'tensor')), may hold values from -6 to 6
- segment_ids: int32 [2, 16384], replicated, may hold values from 0 to 11, as said below
- w_qkv: bfloat16 [1280, 3, 1280], P('dp', None, 'tensor'), may hold values from -0.15625 to 0.15625
- w_out: bfloat16 [1280, 1280], P('dp', 'tensor'), may hold values from -4 to 4
- w_fc1: bfloat16 [1280, 5120], P('dp', 'tensor'), may hold values from -0.15625 to 0.15625
- w_fc2: bfloat16 [1280, 5120], P('dp', 'tensor'), may hold values from -0.078125 to 0.078125
- bias_qv: bfloat16 [2, 1280], P(None, 'tensor'), may hold values from -2 to 2
- bias_fc1: bfloat16 [5120], P('tensor'), may hold values from -3 to 3
- norm_vectors: bfloat16 [6, 1280], replicated, may hold values from -1.2 to 1.6
Outputs:
- output: bfloat16 [2, 16384, 1280], P(None, ('dp', 'tensor'))
- frames_grad: float32 [2, 16384, 1280], P(None, ('dp', 'tensor'))
- grad_qkv: float32 [1280, 3, 1280], P('dp', None, 'tensor')
- grad_out: float32 [1280, 1280], P('dp', 'tensor')
- grad_fc1: float32 [1280, 5120], P('dp', 'tensor')
- grad_fc2: float32 [1280, 5120], P('dp', 'tensor')
- grad_bias_qv: float32 [2, 1280], P(None, 'tensor')
- grad_bias_fc1: float32 [5120], P('tensor')
- grad_norm: float32 [6, 1280], replicated
The draws below stay inside these ranges and needn't reach their ends.
Inputs may be any that keep to these rules, and one draw needn't show every extreme that they name: `segment_ids`: each micro-batch's row numbers its clips 0, 1, 2, ... in order of frames, never falling; every clip has at most 1500 frames, and in every micro-batch one clip has exactly 1500.
All inputs are finite; a program needn't handle non-finite values.
Results may differ from the reference program's by a relative error of at most 0.02.
Values may be sent and summed in bfloat16 or wider, within the bound.
No kernel may reach another device: no remote copies, remote signals or barrier semaphores. Data moves between devices by JAX's collectives and lax.ppermute only.
A program may use at most 264 MiB of HBM per device.

```python
import math
import jax
import jax.numpy as jnp
from jax import lax

D = 1280
H = 16
FF = 5120
HD = 80
MB = 2
CLIP_MAX = 1500
CLIP_MIN = 1024
CLIP_MEAN = 1280
MBTOK = 16384


def draw_segment_ids(key, part):
    clip_count = MBTOK // CLIP_MEAN
    base_len = MBTOK // clip_count
    leftover = MBTOK - base_len * clip_count
    pair_count = clip_count // 2
    swing_room = min(CLIP_MAX - base_len - 1, base_len - CLIP_MIN)
    first_len = base_len + (1 if leftover > 0 else 0)
    clip_index = jnp.arange(clip_count, dtype=jnp.int32)
    starting = base_len + (clip_index < leftover).astype(jnp.int32)
    frame_pos = jnp.arange(MBTOK, dtype=jnp.int32)
    rows_out = []
    for number in range(MB):
        batch_key = jax.random.fold_in(key, number)
        key_swing, key_roll = jax.random.split(batch_key)
        swing = jax.random.randint(key_swing, (pair_count,), 0, swing_room + 1, dtype=jnp.int32)
        swing = swing.at[0].set(CLIP_MAX - first_len)
        changes = jnp.zeros((clip_count,), jnp.int32)
        changes = changes.at[0:2 * pair_count:2].set(swing)
        changes = changes.at[1:2 * pair_count:2].set(-swing)
        lengths = jnp.roll(starting + changes, jax.random.randint(key_roll, (), 0, clip_count, dtype=jnp.int32))
        clip_ends = jnp.cumsum(lengths)
        rows_out.append(jnp.sum((frame_pos[:, None] >= clip_ends[None, :]).astype(jnp.int32), axis=1))
    return jnp.stack(rows_out)


def draw_bias_qv(key, part):
    scales = jnp.array([[0.5], [0.03]], jnp.float32)
    noise_rows = jnp.clip(jax.random.normal(key, (2, D), jnp.float32), -4.0, 4.0)
    return (noise_rows * scales).astype(jnp.bfloat16)


def draw_norm_vectors(key, part):
    centre = jnp.array([[1.0], [0.0], [1.0], [0.0], [0.0], [0.0]], jnp.float32)
    scales = jnp.array([[0.15], [0.3], [0.15], [0.3], [0.3], [0.3]], jnp.float32)
    noise_rows = jnp.clip(jax.random.normal(key, (6, D), jnp.float32), -4.0, 4.0)
    return (centre + noise_rows * scales).astype(jnp.bfloat16)


def levels(own_key, shape, cuts, smallest, top_value):
    def one(position, shards_of):
        steps = jax.random.uniform(jax.random.fold_in(jax.random.fold_in(own_key, 6), position), (shards_of,), jnp.float32, smallest / len(cuts), top_value / len(cuts))
        return jnp.repeat(jnp.exp(steps), shape[position] // shards_of).reshape((-1,) + (1,) * (len(shape) - position - 1))

    level = one(*cuts[0])
    for cut in cuts[1:]:
        level = level * one(*cut)
    return level


def gaussian(rng, dims, deviation, reach, cuts=(), kind=jnp.bfloat16):
    entries = jax.random.normal(rng, dims, jnp.float32) * deviation
    if len(cuts) > 0:
        entries = levels(rng, dims, cuts, -0.22, 0.18) * entries
    return jnp.clip(entries, min=-reach, max=reach).astype(kind)


def setup_inputs(seed: int = 0) -> dict:
    seeds = jax.random.split(jax.random.key(seed), 11)
    frames = gaussian(seeds[0], (MB, MBTOK, D), 1.0, 6.0, ((1, 32),))
    cotangent = gaussian(seeds[1], (MB, MBTOK, D), 1.0, 6.0, ((1, 32),))
    segment_ids = draw_segment_ids(jax.random.fold_in(seeds[10], 71), 0)
    w_qkv = gaussian(seeds[3], (D, 3, D), D ** -0.5, 0.15625, ((0, 16), (2, 2)))
    w_out = gaussian(seeds[4], (D, D), (max(D // 512, 1)) ** -0.5, 4.0, ((0, 16), (1, 2)))
    w_fc1 = gaussian(seeds[5], (D, FF), D ** -0.5, 0.15625, ((0, 16), (1, 2)))
    w_fc2 = gaussian(seeds[6], (D, FF), FF ** -0.5, 0.078125, ((0, 16), (1, 2)))
    bias_qv = draw_bias_qv(jax.random.fold_in(seeds[10], 71), 0)
    bias_fc1 = gaussian(seeds[8], (FF,), 0.5, 3.0, ((0, 2),))
    norm_vectors = draw_norm_vectors(jax.random.fold_in(seeds[10], 71), 0)
    return {"frames": frames, "cotangent": cotangent, "segment_ids": segment_ids, "w_qkv": w_qkv, "w_out": w_out, "w_fc1": w_fc1, "w_fc2": w_fc2, "bias_qv": bias_qv, "bias_fc1": bias_fc1, "norm_vectors": norm_vectors}


EPSILON = 1e-05
NEGATIVE = -1e+30
PRECISE = lax.Precision.HIGHEST

@jax.custom_vjp
def low(v):
    return lax.optimization_barrier(v.astype(jnp.bfloat16)).astype(jnp.float32)

@jax.custom_vjp
def low_back(v):
    return v

def low_keep(v):
    return (low(v), None)

def low_pass(kept, grad):
    return (grad,)

def back_keep(v):
    return (v, None)

def back_low(kept, grad):
    return (low(grad),)
low.defvjp(low_keep, low_pass)
low_back.defvjp(back_keep, back_low)

def round_both(values):
    return low(low_back(values))

def norm_rows(values, gain, shift):
    average = lax.optimization_barrier(jnp.mean(values, axis=-1, keepdims=True))
    centred = values - average
    spread = lax.optimization_barrier(jnp.mean(centred * centred, axis=-1, keepdims=True))
    return centred * lax.rsqrt(spread + EPSILON) * gain + shift

def attend(queries, key_rows, val_rows, clip_ids):
    length = queries.shape[0]
    block_len = math.gcd(length, 1024)
    span_len = block_len + 2 * CLIP_MAX
    score_scale = 1.0 / math.sqrt(HD)
    padded_keys = jnp.pad(key_rows, ((CLIP_MAX, CLIP_MAX), (0, 0), (0, 0)))
    padded_vals = jnp.pad(val_rows, ((CLIP_MAX, CLIP_MAX), (0, 0), (0, 0)))
    padded_ids = jnp.pad(clip_ids, (CLIP_MAX, CLIP_MAX), constant_values=-1)

    def one_block(start_row):
        query_block = lax.dynamic_slice_in_dim(queries, start_row, block_len, 0)
        ids_query = lax.dynamic_slice_in_dim(clip_ids, start_row, block_len, 0)
        key_block = lax.dynamic_slice_in_dim(padded_keys, start_row, span_len, 0)
        val_block = lax.dynamic_slice_in_dim(padded_vals, start_row, span_len, 0)
        ids_block = lax.dynamic_slice_in_dim(padded_ids, start_row, span_len, 0)
        raw_scores = low_back(jnp.einsum('qhd,khd->hqk', query_block, key_block, precision=PRECISE) * score_scale)
        same_clip = (ids_query[:, None] == ids_block[None, :])[None]
        masked = jnp.where(same_clip, raw_scores, NEGATIVE)
        row_top = lax.optimization_barrier(jnp.max(masked, axis=-1, keepdims=True))
        expo_rows = jnp.exp(masked - row_top)
        prob_rows = expo_rows / lax.optimization_barrier(jnp.sum(expo_rows, axis=-1, keepdims=True))
        return jnp.einsum('hqk,khd->qhd', low(prob_rows), val_block, precision=PRECISE)
    starts = jnp.arange(length // block_len, dtype=jnp.int32) * block_len
    blocks_out = lax.map(jax.checkpoint(one_block), starts)
    return blocks_out.reshape(length, queries.shape[1] * queries.shape[2])

def layer_pass(frame_rows, clip_ids, params):
    w_qkv, w_out, w_fc1, w_fc2, bias_qv, bias_fc1, vectors = params
    normed_one = low(norm_rows(frame_rows, vectors[0], vectors[1]))
    projected = jnp.einsum('sd,dtc->stc', normed_one, w_qkv, precision=PRECISE)
    queries = round_both(projected[:, 0] + bias_qv[0]).reshape(-1, H, HD)
    key_rows = round_both(projected[:, 1]).reshape(-1, H, HD)
    val_rows = round_both(projected[:, 2] + bias_qv[1]).reshape(-1, H, HD)
    mixed = round_both(attend(queries, key_rows, val_rows, clip_ids))
    middle = frame_rows + low_back(jnp.einsum('sc,dc->sd', mixed, w_out, precision=PRECISE)) + vectors[4]
    normed_two = low(norm_rows(middle, vectors[2], vectors[3]))
    hidden = low_back(jnp.dot(normed_two, w_fc1, precision=PRECISE, preferred_element_type=jnp.float32) + bias_fc1)
    active = low(jax.nn.gelu(hidden, approximate=False))
    return middle + low_back(jnp.einsum('sf,df->sd', active, w_fc2, precision=PRECISE)) + vectors[5]

def reference(frames, cotangent, segment_ids, w_qkv, w_out, w_fc1, w_fc2, bias_qv, bias_fc1, norm_vectors):
    params = tuple((weight.astype(jnp.float32) for weight in (w_qkv, w_out, w_fc1, w_fc2, bias_qv, bias_fc1, norm_vectors)))
    totals = tuple((jnp.zeros_like(weight) for weight in params))
    outputs = []
    inputs_grad = []
    for number in range(MB):
        clip_ids = segment_ids[number]

        def run_layer(frame_rows, weights, clip_ids=clip_ids):
            return layer_pass(frame_rows, clip_ids, weights)
        result, pull_back = jax.vjp(run_layer, frames[number].astype(jnp.float32), params)
        grad_frames, grad_params = pull_back(cotangent[number].astype(jnp.float32))
        outputs.append(result.astype(jnp.bfloat16))
        inputs_grad.append(grad_frames)
        totals = tuple((running + update for running, update in zip(totals, grad_params)))
    return (jnp.stack(outputs), jnp.stack(inputs_grad), totals[0], totals[1], totals[2], totals[3], totals[4], totals[5], totals[6])
```

```python
import functools
import math

import jax
import jax.numpy as jnp
from jax import lax
from jax.experimental import pallas as pl
from jax.experimental.pallas import tpu as pltpu
from jax.sharding import PartitionSpec as P

HD = 80
MB = 2
EDGE = 512
EPSILON = 1e-05
NEGATIVE = -1e30
LOG2E = math.log2(math.e)
SCALE = 1.0 / math.sqrt(HD)
BF = jnp.bfloat16
F32 = jnp.float32


def head_spans(heads):
    spans = []
    for head in range(heads):
        first, last = head * HD, (head + 1) * HD
        start = first // 128 * 128
        spans.append((start, -(-last // 128) * 128 - start, first - start))
    return spans


def dot_on(a, b, a_dim, b_dim):
    return lax.dot_general(a, b, (((a_dim,), (b_dim,)), ((), ())), preferred_element_type=F32)


def in_head(rows, width, offset):
    lane = lax.broadcasted_iota(jnp.int32, (rows, width), 1)
    return (lane >= offset) & (lane < offset + HD)


def head_ones(width, offset):
    return jnp.where(in_head(1, width, offset), 1.0, 0.0).astype(BF)


def window_parts(refs, swap):
    parts, base = [], 0
    for ref in refs:
        rows = ref.shape[0]
        if rows == EDGE:
            parts.append((ref, 0, base, rows))
        else:
            half = rows // 2
            parts.append((ref, 0, base + swap * half, half))
            parts.append((ref, half, base + (1 - swap) * half, half))
        base += rows
    return parts


def fetch_window(refs, swap, window, sems):
    copies = []
    for number, (ref, row, at, rows) in enumerate(window_parts(refs, swap)):
        copies.append(
            pltpu.make_async_copy(
                ref.at[pl.ds(row, rows)],
                window.at[pl.ds(pl.multiple_of(at, EDGE), rows)],
                sems.at[number],
            )
        )
        copies[-1].start()
    for copy in copies:
        copy.wait()


def forward_kernel(
    heads, W, QB, KB, lo_ref, count_ref, swap_ref, st_ref, en_ref, q_ref, l2, l1, own, r1, r2,
    o_ref, lse_ref, window, sems, top_s, sum_s, acc_s,
):
    fetch_window((l2, l1, own, r1, r2), swap_ref[0], window, sems)
    spans = head_spans(heads)

    def query_block(i, carry):
        r = pl.multiple_of(i * QB, QB)
        top_s[...] = jnp.full(top_s.shape, NEGATIVE, F32)
        sum_s[...] = jnp.zeros(sum_s.shape, F32)
        acc_s[...] = jnp.zeros(acc_s.shape, F32)
        st = st_ref[pl.ds(r, QB), :]
        en = en_ref[pl.ds(r, QB), :]

        def chunk(c, inner):
            k0 = pl.multiple_of(lo_ref[i] + c * KB, 16)
            at = k0 + lax.broadcasted_iota(jnp.int32, (QB, KB), 1)
            mask = (at >= st) & (at < en)
            for h in range(heads):
                t, w, off = spans[h]
                q = q_ref[pl.ds(r, QB), t : t + w] * head_ones(w, off)
                s = dot_on(q, window[pl.ds(k0, KB), t : t + w], 1, 1)
                s = jnp.where(mask, s, NEGATIVE)
                before = top_s[h]
                top = jnp.maximum(before, jnp.max(s, axis=1, keepdims=True))
                p = jnp.exp2(s - top)
                shrink = jnp.exp2(before - top)
                sum_s[h] = sum_s[h] * shrink + jnp.sum(p, axis=1, keepdims=True)
                acc_s[h, :, :w] = acc_s[h, :, :w] * shrink + dot_on(
                    p.astype(BF), window[pl.ds(k0, KB), W + t : W + t + w], 1, 0
                )
                top_s[h] = top
            return inner

        lax.fori_loop(0, count_ref[i], chunk, 0)
        for h in range(heads):
            t, w, off = spans[h]
            total = sum_s[h]
            o = (acc_s[h, :, :w] / total).astype(BF)
            o_ref[pl.ds(r, QB), t : t + w] = jnp.where(
                in_head(QB, w, off), o, o_ref[pl.ds(r, QB), t : t + w]
            )
            lse_ref[pl.ds(r, QB), h : h + 1] = top_s[h] + jnp.log2(total)
        return carry

    lax.fori_loop(0, q_ref.shape[0] // QB, query_block, 0)


SMEM = pl.BlockSpec(memory_space=pltpu.SMEM)
VMEM = pl.BlockSpec(memory_space=pltpu.VMEM)
ANY = pl.BlockSpec(memory_space=pl.ANY)


def attend_forward(q, pieces, ranges, swap, heads, QB=256, KB=768):
    st, en = ranges
    FR, W = q.shape
    rows = sum(p.shape[0] for p in pieces)
    lo, count = key_chunks(st, en, QB, KB, rows)
    flops = 2 * 2 * FR * 1792 * 256 * heads
    return pl.pallas_call(
        functools.partial(forward_kernel, heads, W, QB, KB),
        out_shape=(
            jax.ShapeDtypeStruct((FR, W), BF),
            jax.ShapeDtypeStruct((FR, heads), F32),
        ),
        in_specs=[SMEM] * 3 + [VMEM] * 3 + [ANY] * 5,
        out_specs=(VMEM, VMEM),
        scratch_shapes=[
            pltpu.VMEM((rows, 2 * W), BF),
            pltpu.SemaphoreType.DMA((8,)),
            pltpu.VMEM((heads, QB, 1), F32),
            pltpu.VMEM((heads, QB, 1), F32),
            pltpu.VMEM((heads, QB, 256), F32),
        ],
        compiler_params=pltpu.CompilerParams(vmem_limit_bytes=56 << 20),
        cost_estimate=pl.CostEstimate(flops=flops * 4, bytes_accessed=rows * W * 4, transcendentals=0),
        name="attend_forward",
    )(lo, count, swap[None], st[:, None], en[:, None], q, *pieces)


def backward_kernel(
    heads, W, QB, KB, lo_ref, count_ref, swap_ref, se_ref, lse_ref, delta_ref, q_ref, do_ref,
    l2, l1, own, r1, r2, dq_ref, g_l2, g_l1, g_own, g_r1, g_r2, window, grads, dq_s, sems,
):
    swap = swap_ref[0]
    fetch_window((l2, l1, own, r1, r2), swap, window, sems)
    spans = head_spans(heads)
    grads[...] = jnp.zeros(grads.shape, F32)

    def query_block(i, carry):
        r = pl.multiple_of(i * QB, QB)
        dq_s[...] = jnp.zeros(dq_s.shape, F32)
        st = se_ref[0:1, pl.ds(r, QB)]
        en = se_ref[1:2, pl.ds(r, QB)]

        def chunk(c, inner):
            k0 = pl.multiple_of(lo_ref[i] + c * KB, 16)
            at = k0 + lax.broadcasted_iota(jnp.int32, (KB, QB), 0)
            mask = (at >= st) & (at < en)
            for h in range(heads):
                t, w, off = spans[h]
                ones = head_ones(w, off)
                q = q_ref[pl.ds(r, QB), t : t + w] * ones
                do = do_ref[pl.ds(r, QB), t : t + w] * ones
                k = window[pl.ds(k0, KB), t : t + w]
                v = window[pl.ds(k0, KB), W + t : W + t + w]
                s = dot_on(k, q, 1, 1)
                p = jnp.exp2(jnp.where(mask, s - lse_ref[h : h + 1, pl.ds(r, QB)], NEGATIVE))
                dp = dot_on(v, do, 1, 1)
                ds = (p * (dp - delta_ref[h : h + 1, pl.ds(r, QB)])).astype(BF)
                grads[pl.ds(k0, KB), W + t : W + t + w] += dot_on(p.astype(BF), do, 1, 0)
                grads[pl.ds(k0, KB), t : t + w] += dot_on(ds, q, 1, 0)
                dq_s[h, :, :w] += dot_on(ds, k, 0, 0)
            return inner

        lax.fori_loop(0, count_ref[i], chunk, 0)
        for h in range(heads):
            t, w, off = spans[h]
            dq = (dq_s[h, :, :w] * SCALE).astype(BF)
            dq_ref[pl.ds(r, QB), t : t + w] = jnp.where(
                in_head(QB, w, off), dq, dq_ref[pl.ds(r, QB), t : t + w]
            )
        return carry

    lax.fori_loop(0, q_ref.shape[0] // QB, query_block, 0)
    for ref, row, at, rows in window_parts((g_l2, g_l1, g_own, g_r1, g_r2), swap):

        def store(j, carry, ref=ref, row=row, at=at):
            to = pl.multiple_of(row + j * 128, 128)
            here = pl.multiple_of(at + j * 128, 128)
            ref[pl.ds(to, 128), :W] = (grads[pl.ds(here, 128), :W] * math.log(2.0)).astype(BF)
            ref[pl.ds(to, 128), W:] = grads[pl.ds(here, 128), W:].astype(BF)
            return carry

        lax.fori_loop(0, rows // 128, store, 0)


def attend_backward(q, do, pieces, ranges, lse, delta, swap, heads, QB=256, KB=768):
    st, en = ranges
    FR, W = q.shape
    rows = sum(p.shape[0] for p in pieces)
    lo, count = key_chunks(st, en, QB, KB, rows)
    flops = 5 * 2 * FR * 1792 * 256 * heads
    return pl.pallas_call(
        functools.partial(backward_kernel, heads, W, QB, KB),
        out_shape=(jax.ShapeDtypeStruct((FR, W), BF),)
        + tuple(jax.ShapeDtypeStruct(p.shape, BF) for p in pieces),
        in_specs=[SMEM] * 3 + [VMEM] * 5 + [ANY] * 5,
        out_specs=(VMEM,) * 6,
        scratch_shapes=[
            pltpu.VMEM((rows, 2 * W), BF),
            pltpu.VMEM((rows, 2 * W), F32),
            pltpu.VMEM((heads, QB, 256), F32),
            pltpu.SemaphoreType.DMA((8,)),
        ],
        compiler_params=pltpu.CompilerParams(vmem_limit_bytes=60 << 20),
        cost_estimate=pl.CostEstimate(flops=flops * 2, bytes_accessed=rows * W * 8, transcendentals=0),
        name="attend_backward",
    )(lo, count, swap[None], jnp.stack((st, en)), lse, delta, q, do, *pieces)


def key_chunks(st, en, QB, KB, rows):
    lo = st[::QB] // 16 * 16
    count = (en[QB - 1 :: QB] - lo + KB - 1) // KB
    return jnp.minimum(lo, rows - count * KB), count


def over_dp(x, by):
    length = lax.axis_size("dp")
    pairs = [(i, i + by) for i in range(length) if 0 <= i + by < length]
    return lax.ppermute(x, "dp", pairs)


def partner(x):
    return lax.ppermute(x, "tensor", [(0, 1), (1, 0)])


def collect(x):
    if lax.axis_size("tensor") != 2:
        return lax.all_gather(x, "tensor", axis=0, tiled=True)
    return jnp.concatenate((x, partner(x)), axis=0)


def summed(parts):
    def product(first, last):
        return sum(dot_on(x[first:last], w, 1, dim) for x, w, dim in parts)

    rows = parts[0][0].shape[0]
    if lax.axis_size("tensor") != 2:
        whole = product(0, rows).astype(BF)
        return lax.psum_scatter(whole, "tensor", scatter_dimension=0, tiled=True).astype(F32)
    half = rows // 2
    received = partner(product(half, rows).astype(BF))
    return product(0, half) + received.astype(F32)


def norm_parts(x):
    centred = x - jnp.mean(x, axis=-1, keepdims=True)
    scale = lax.rsqrt(jnp.mean(centred * centred, axis=-1, keepdims=True) + EPSILON)
    return centred * scale, scale


def norm_back(grad, z, scale, gain):
    e = grad * gain
    mean_e = jnp.mean(e, axis=-1, keepdims=True)
    mean_ez = jnp.mean(e * z, axis=-1, keepdims=True)
    return scale * (e - mean_e - z * mean_ez)


def gelu_both(u):
    below = 0.5 * (1.0 + lax.erf(u * math.sqrt(0.5)))
    density = jnp.exp(-0.5 * u * u) * (1.0 / math.sqrt(2.0 * math.pi))
    return (u * below).astype(BF), (below + u * density).astype(BF)


def per_device(
    frames, cotangent, segment_ids, w_qkv, w_out, w_fc1, w_fc2, bias_qv, bias_fc1, norm_vectors
):
    dp_place = lax.axis_index("dp")
    paired = lax.axis_size("tensor") == 2
    swap = lax.axis_index("tensor").astype(jnp.int32) if paired else jnp.int32(0)
    own = frames.shape[1]
    FR = own * lax.axis_size("tensor")
    half = FR // 2
    rows = 2 * EDGE + 3 * FR
    local = w_qkv.shape[2]
    heads = local // HD
    W = -(-local // 128) * 128
    fill = W - local
    vectors = norm_vectors.astype(F32)

    def widened(x):
        return jnp.pad(x, [(0, 0)] * (x.ndim - 1) + [(0, fill)]) if fill else x

    def gathered(w):
        return lax.all_gather(w, "dp", axis=0, tiled=True)

    qkv_all = gathered(widened(w_qkv).reshape(w_qkv.shape[0], 3 * W))
    out_all = gathered(widened(w_out))
    fc1_all = gathered(w_fc1)
    fc2_all = gathered(w_fc2)
    wq, wkv = qkv_all[:, :W], qkv_all[:, W:]
    bias_q = widened(bias_qv[0].astype(F32))
    bias_kv = jnp.concatenate((jnp.zeros((W,), F32), widened(bias_qv[1].astype(F32))))

    z1s, r1s, h1s, qs, pieces, ranges, mixeds, lses = [], [], [], [], [], [], [], []
    for b in range(MB):
        z1, r1 = norm_parts(frames[b].astype(F32))
        h1 = collect((z1 * vectors[0] + vectors[1]).astype(BF))
        q = ((dot_on(h1, wq, 1, 0) + bias_q) * (LOG2E * SCALE)).astype(BF)
        kv = (dot_on(h1, wkv, 1, 0) + bias_kv).astype(BF)
        head = lax.dynamic_slice_in_dim(kv, swap * half, EDGE)
        tail = lax.dynamic_slice_in_dim(kv, (1 - swap) * half, EDGE)
        pieces.append((over_dp(tail, 2), over_dp(kv, 1), kv, over_dp(kv, -1), over_dp(head, -2)))
        ids = segment_ids[b]
        reach = FR + EDGE
        padded = jnp.concatenate(
            (jnp.full((reach,), -1, jnp.int32), ids, jnp.full((reach,), 1 << 30, jnp.int32))
        )
        near = lax.dynamic_slice_in_dim(padded, dp_place * FR, rows)
        mine = jnp.concatenate(
            (
                lax.dynamic_slice_in_dim(ids, dp_place * FR + swap * half, half),
                lax.dynamic_slice_in_dim(ids, dp_place * FR + (1 - swap) * half, half),
            )
        )
        st = jnp.sum((near[None, :] < mine[:, None]).astype(jnp.int32), axis=1)
        en = jnp.sum((near[None, :] <= mine[:, None]).astype(jnp.int32), axis=1)
        z1s.append(z1)
        r1s.append(r1)
        h1s.append(h1)
        qs.append(q)
        ranges.append((st, en))

    middles, h2s, actives, slopes, outputs = [], [], [], [], []
    for b in range(MB):
        mixed, lse = attend_forward(qs[b], pieces[b], ranges[b], swap, heads)
        middle = frames[b].astype(F32) + summed([(mixed, out_all, 1)]) + vectors[4]
        z2, r2 = norm_parts(middle)
        h2 = collect((z2 * vectors[2] + vectors[3]).astype(BF))
        hidden = dot_on(h2, fc1_all, 1, 0) + bias_fc1.astype(F32)
        active, slope = gelu_both(hidden)
        result = middle + summed([(active, fc2_all, 1)]) + vectors[5]
        outputs.append(result.astype(BF))
        mixeds.append(mixed)
        lses.append(lse)
        middles.append(middle)
        h2s.append(h2)
        actives.append(active)
        slopes.append(slope)

    term_fc2 = term_fc1 = term_out = term_q = term_kv = 0.0
    bias_q_sum = bias_v_sum = bias_fc1_sum = 0.0
    norm_sums = 0.0
    inputs_grad = []
    for b in range(MB):
        grad_rows = cotangent[b].astype(F32)
        grad_f = collect(cotangent[b])
        grad_hidden = (dot_on(grad_f, fc2_all, 1, 0) * slopes[b].astype(F32)).astype(BF)
        term_fc2 = term_fc2 + dot_on(grad_f, actives[b], 0, 0)
        bias_fc1_sum = bias_fc1_sum + jnp.sum(grad_hidden, axis=0, dtype=F32)
        term_fc1 = term_fc1 + dot_on(h2s[b], grad_hidden, 0, 0)
        grad_h2 = summed([(grad_hidden, fc1_all, 1)])
        z2, r2 = norm_parts(middles[b])
        grad_middle = grad_rows + norm_back(grad_h2, z2, r2, vectors[2])
        grad_a = collect(grad_middle.astype(BF))
        term_out = term_out + dot_on(grad_a, mixeds[b], 0, 0)
        grad_mixed = dot_on(grad_a, out_all, 1, 0).astype(BF)
        chosen = (jnp.arange(W)[:, None] // HD == jnp.arange(heads)[None, :]).astype(F32)
        delta = lax.dot_general(
            chosen,
            grad_mixed.astype(F32) * mixeds[b].astype(F32),
            (((0,), (1,)), ((), ())),
            precision=lax.Precision.HIGHEST,
        )
        grad_q, g_l2, g_l1, g_own, g_r1, g_r2 = attend_backward(
            qs[b], grad_mixed, pieces[b], ranges[b], lses[b].T, delta, swap, heads
        )
        to_tail = over_dp(g_l2, -2).astype(F32)
        to_head = over_dp(g_r2, 2).astype(F32)
        first = jnp.where(swap == 1, to_tail, to_head)
        second = jnp.where(swap == 1, to_head, to_tail)
        grad_kv = (
            g_own.astype(F32)
            + over_dp(g_l1, -1).astype(F32)
            + over_dp(g_r1, 1).astype(F32)
            + jnp.concatenate((first, second))
        ).astype(BF)
        bias_q_sum = bias_q_sum + jnp.sum(grad_q, axis=0, dtype=F32)
        bias_v_sum = bias_v_sum + jnp.sum(grad_kv[:, W:], axis=0, dtype=F32)
        term_q = term_q + dot_on(h1s[b], grad_q, 0, 0)
        term_kv = term_kv + dot_on(h1s[b], grad_kv, 0, 0)
        grad_h1 = summed([(grad_q, wq, 1), (grad_kv, wkv, 1)])
        inputs_grad.append(grad_middle + norm_back(grad_h1, z1s[b], r1s[b], vectors[0]))
        norm_sums = norm_sums + jnp.stack(
            (
                jnp.sum(grad_h1 * z1s[b], axis=0),
                jnp.sum(grad_h1, axis=0),
                jnp.sum(grad_h2 * z2, axis=0),
                jnp.sum(grad_h2, axis=0),
                jnp.sum(grad_middle, axis=0),
                jnp.sum(grad_rows, axis=0),
            )
        )

    def owned(term):
        return lax.psum_scatter(term.astype(BF), "dp", scatter_dimension=0, tiled=True).astype(F32)

    own_fc2 = owned(term_fc2)
    own_fc1 = owned(term_fc1)
    own_out = owned(term_out)[:, :local]
    own_qkv = owned(jnp.concatenate((term_q, term_kv), axis=1))
    own_qkv = own_qkv.reshape(own_qkv.shape[0], 3, W)[:, :, :local]
    bias_total = lax.psum((jnp.stack((bias_q_sum, bias_v_sum))[:, :local], bias_fc1_sum), "dp")
    norm_total = lax.psum(norm_sums, ("dp", "tensor"))
    return (
        jnp.stack(outputs),
        jnp.stack(inputs_grad),
        own_qkv,
        own_out,
        own_fc1,
        own_fc2,
        bias_total[0],
        bias_total[1],
        norm_total,
    )


def solution(mesh):
    in_specs = (
        P(None, ("dp", "tensor"), None),
        P(None, ("dp", "tensor"), None),
        P(),
        P("dp", None, "tensor"),
        P("dp", "tensor"),
        P("dp", "tensor"),
        P("dp", "tensor"),
        P(None, "tensor"),
        P("tensor"),
        P(),
    )
    out_specs = (
        P(None, ("dp", "tensor"), None),
        P(None, ("dp", "tensor"), None),
        P("dp", None, "tensor"),
        P("dp", "tensor"),
        P("dp", "tensor"),
        P("dp", "tensor"),
        P(None, "tensor"),
        P("tensor"),
        P(),
    )
    return jax.shard_map(
        per_device, mesh=mesh, in_specs=in_specs, out_specs=out_specs, check_vma=False
    )
```

```python
import functools
import math

import jax
import jax.numpy as jnp
from jax import lax
from jax.experimental import pallas as pl
from jax.experimental.pallas import tpu as pltpu
from jax.sharding import PartitionSpec as P

HD = 80
MB = 2
EDGE = 512
EPSILON = 1e-05
NEGATIVE = -1e30
LOG2E = math.log2(math.e)
SCALE = 1.0 / math.sqrt(HD)
BF = jnp.bfloat16
F32 = jnp.float32


def head_spans(heads):
    spans = []
    for head in range(heads):
        first, last = head * HD, (head + 1) * HD
        start = first // 128 * 128
        spans.append((start, -(-last // 128) * 128 - start, first - start))
    return spans


def dot_on(a, b, a_dim, b_dim):
    return lax.dot_general(a, b, (((a_dim,), (b_dim,)), ((), ())), preferred_element_type=F32)


def in_head(rows, width, offset):
    lane = lax.broadcasted_iota(jnp.int32, (rows, width), 1)
    return (lane >= offset) & (lane < offset + HD)


def head_ones(width, offset):
    return jnp.where(in_head(1, width, offset), 1.0, 0.0).astype(BF)


def window_parts(refs, swap, FR):
    half = FR // 2
    both = (swap * half, (1 - swap) * half)
    bases = [[base + add for add in both] for base in (EDGE, EDGE + FR, EDGE + 2 * FR)]
    bases = [[0]] + bases + [[EDGE + 3 * FR]]
    return [
        (ref, number * half, base, half)
        for ref, group in zip(refs, bases)
        for number, base in enumerate(group)
    ]


def fetch_window(refs, place, FR, window, sems):
    swap, core = place[0], place[1]
    left_direct, left_relayed, *near, right_direct, right_relayed = refs
    copies = []
    for number, (ref, row, at, rows) in enumerate(window_parts([left_direct, *near, right_direct], swap, FR)):
        to = window.at[pl.ds(pl.multiple_of(at, EDGE), rows)]
        copies.append(pltpu.make_async_copy(ref.at[pl.ds(row, rows)], to, sems.at[number]))
        if ref is left_direct or ref is right_direct:
            other = pltpu.make_async_copy(
                left_relayed if ref is left_direct else right_relayed, to, sems.at[number]
            )
            here = core == (0 if ref is left_direct else 1)
            pl.when(here)(copies[-1].start)
            pl.when(jnp.logical_not(here))(other.start)
        else:
            copies[-1].start()
    for copy in copies:
        copy.wait()


def forward_kernel(heads, W, QB, KB, lo_ref, count_ref, place_ref, se_ref, q_ref, *refs):
    *pieces, o_ref, lse_ref, window, sems, top_s, sum_s, acc_s = refs
    fetch_window(pieces, place_ref, q_ref.shape[0], window, sems)
    spans = head_spans(heads)

    def query_block(i, carry):
        r = pl.multiple_of(i * QB, QB)
        top_s[...] = jnp.full(top_s.shape, NEGATIVE, F32)
        sum_s[...] = jnp.zeros(sum_s.shape, F32)
        acc_s[...] = jnp.zeros(acc_s.shape, F32)
        st = se_ref[0:1, pl.ds(r, QB)]
        en = se_ref[1:2, pl.ds(r, QB)]

        def chunk(c, inner):
            k0 = pl.multiple_of(lo_ref[i] + c * KB, 16)
            at = k0 + lax.broadcasted_iota(jnp.int32, (KB, QB), 0)
            mask = (at >= st) & (at < en)
            for h in range(heads):
                t, w, off = spans[h]
                q = q_ref[pl.ds(r, QB), t : t + w] * head_ones(w, off)
                v = window[pl.ds(k0, KB), W + t : W + t + w]
                s = dot_on(window[pl.ds(k0, KB), t : t + w], q, 1, 1)
                s = jnp.where(mask, s, NEGATIVE)
                before = top_s[h : h + 1, :]
                top = jnp.maximum(before, jnp.max(s, axis=0, keepdims=True))
                p = jnp.exp2(s - top)
                shrink = jnp.exp2(before - top)
                sum_s[h : h + 1, :] = sum_s[h : h + 1, :] * shrink + jnp.sum(p, axis=0, keepdims=True)
                acc_s[h, :w, :] = acc_s[h, :w, :] * shrink + dot_on(v, p.astype(BF), 0, 0)
                top_s[h : h + 1, :] = top
            return inner

        lax.fori_loop(0, count_ref[i], chunk, 0)
        for h in range(heads):
            t, w, off = spans[h]
            o = (acc_s[h, :w, :] / sum_s[h : h + 1, :]).T.astype(BF)
            o_ref[pl.ds(r, QB), t : t + w] = jnp.where(
                in_head(QB, w, off), o, o_ref[pl.ds(r, QB), t : t + w]
            )
        lse_ref[:, pl.ds(r, QB)] = top_s[...] + jnp.log2(sum_s[...])
        return carry

    lax.fori_loop(0, q_ref.shape[0] // QB, query_block, 0)


SMEM = pl.BlockSpec(memory_space=pltpu.SMEM)
VMEM = pl.BlockSpec(memory_space=pltpu.VMEM)
ANY = pl.BlockSpec(memory_space=pl.ANY)


def attend_forward(q, pieces, ranges, swap, heads, QB=256, KB=768):
    st, en = ranges
    FR, W = q.shape
    rows = 3 * FR + 2 * EDGE
    lo, count = key_chunks(st, en, QB, KB, rows)
    return pl.pallas_call(
        functools.partial(forward_kernel, heads, W, QB, KB),
        out_shape=(
            jax.ShapeDtypeStruct((FR, W), BF),
            jax.ShapeDtypeStruct((heads, FR), F32),
        ),
        in_specs=[SMEM] * 3 + [VMEM] * 2 + [ANY] * len(pieces),
        out_specs=(VMEM, VMEM),
        scratch_shapes=[
            pltpu.VMEM((rows, 2 * W), BF),
            pltpu.SemaphoreType.DMA((8,)),
            pltpu.VMEM((heads, QB), F32),
            pltpu.VMEM((heads, QB), F32),
            pltpu.VMEM((heads, 256, QB), F32),
        ],
        compiler_params=pltpu.CompilerParams(vmem_limit_bytes=56 << 20),
        cost_estimate=pl.CostEstimate(flops=0, bytes_accessed=0, transcendentals=0),
        name="attend_forward",
    )(lo, count, swap, jnp.stack((st, en)), q, *pieces)


def backward_kernel(
    heads, W, QB, KB, lo_ref, count_ref, swap_ref, se_ref, lse_ref, delta_ref, q_ref, do_ref, *refs
):
    *refs, window, grads, dq_s, sems = refs
    number = len(refs) - 6
    pieces, dq_ref, outs = refs[:number], refs[number], refs[number + 1 :]
    swap = swap_ref[0]
    fetch_window(pieces, swap_ref, q_ref.shape[0], window, sems)
    spans = head_spans(heads)
    grads[...] = jnp.zeros(grads.shape, F32)

    def query_block(i, carry):
        r = pl.multiple_of(i * QB, QB)
        dq_s[...] = jnp.zeros(dq_s.shape, F32)
        st = se_ref[0:1, pl.ds(r, QB)]
        en = se_ref[1:2, pl.ds(r, QB)]

        def chunk(c, inner):
            k0 = pl.multiple_of(lo_ref[i] + c * KB, 16)
            at = k0 + lax.broadcasted_iota(jnp.int32, (KB, QB), 0)
            mask = (at >= st) & (at < en)
            for h in range(heads):
                t, w, off = spans[h]
                ones = head_ones(w, off)
                q = q_ref[pl.ds(r, QB), t : t + w] * ones
                do = do_ref[pl.ds(r, QB), t : t + w] * ones
                k = window[pl.ds(k0, KB), t : t + w]
                v = window[pl.ds(k0, KB), W + t : W + t + w]
                s = dot_on(k, q, 1, 1)
                p = jnp.exp2(jnp.where(mask, s - lse_ref[h : h + 1, pl.ds(r, QB)], NEGATIVE))
                dp = dot_on(v, do, 1, 1)
                ds = (p * (dp - delta_ref[h : h + 1, pl.ds(r, QB)])).astype(BF)
                grads[pl.ds(k0, KB), W + t : W + t + w] += dot_on(p.astype(BF), do, 1, 0)
                grads[pl.ds(k0, KB), t : t + w] += dot_on(ds, q, 1, 0)
                dq_s[h, :, :w] += dot_on(ds, k, 0, 0)
            return inner

        lax.fori_loop(0, count_ref[i], chunk, 0)
        for h in range(heads):
            t, w, off = spans[h]
            dq = (dq_s[h, :, :w] * SCALE).astype(BF)
            dq_ref[pl.ds(r, QB), t : t + w] = jnp.where(
                in_head(QB, w, off), dq, dq_ref[pl.ds(r, QB), t : t + w]
            )
        return carry

    lax.fori_loop(0, q_ref.shape[0] // QB, query_block, 0)
    for ref, row, at, rows in window_parts(outs, swap, q_ref.shape[0]):

        def store(j, carry, ref=ref, row=row, at=at):
            to = pl.multiple_of(row + j * 128, 128)
            here = pl.multiple_of(at + j * 128, 128)
            ref[pl.ds(to, 128), :W] = (grads[pl.ds(here, 128), :W] * math.log(2.0)).astype(BF)
            ref[pl.ds(to, 128), W:] = grads[pl.ds(here, 128), W:].astype(BF)
            return carry

        lax.fori_loop(0, rows // 128, store, 0)


def attend_backward(q, do, pieces, ranges, lse, delta, swap, heads, QB=256, KB=768):
    st, en = ranges
    FR, W = q.shape
    rows = 3 * FR + 2 * EDGE
    lo, count = key_chunks(st, en, QB, KB, rows)
    grads = [(piece, 2 * W) for piece in (EDGE, FR, FR, FR, EDGE)]
    return pl.pallas_call(
        functools.partial(backward_kernel, heads, W, QB, KB),
        out_shape=(jax.ShapeDtypeStruct((FR, W), BF),)
        + tuple(jax.ShapeDtypeStruct(shape, BF) for shape in grads),
        in_specs=[SMEM] * 3 + [VMEM] * 5 + [ANY] * len(pieces),
        out_specs=(VMEM,) * (1 + len(grads)),
        scratch_shapes=[
            pltpu.VMEM((rows, 2 * W), BF),
            pltpu.VMEM((rows, 2 * W), F32),
            pltpu.VMEM((heads, QB, 256), F32),
            pltpu.SemaphoreType.DMA((8,)),
        ],
        compiler_params=pltpu.CompilerParams(vmem_limit_bytes=60 << 20),
        cost_estimate=pl.CostEstimate(flops=0, bytes_accessed=0, transcendentals=0),
        name="attend_backward",
    )(lo, count, swap, jnp.stack((st, en)), lse, delta, q, do, *pieces)


def key_chunks(st, en, QB, KB, rows):
    lo = st[::QB] // 16 * 16
    count = (en[QB - 1 :: QB] - lo + KB - 1) // KB
    return jnp.minimum(lo, rows - count * KB), count


STEP = 256
FREE = pl.CostEstimate(flops=0, bytes_accessed=0, transcendentals=0)


def once(shape):
    return pl.BlockSpec(shape, lambda i: (0,) * len(shape), pipeline_mode=pl.Buffered(1))


def width_of(n, limit):
    return max(w for w in range(128, min(n, limit) + 1, 128) if n % w == 0)


def dense(xs, weights, n, product, finish, outs, extras=(), name="dense", width=512):
    weight, weight_spec = weights

    def kernel(*refs):
        x_refs, refs = refs[: len(xs)], refs[len(xs) :]
        w_ref, refs = refs[0], refs[1:]
        extra_refs, out_refs = refs[: len(extras)], refs[len(extras) :]
        w = w_ref[...].reshape(w_ref.shape[-2:])
        base = 0
        for x_ref in x_refs:
            for row in range(0, x_ref.shape[0], STEP):
                rows = min(STEP, x_ref.shape[0] - row)
                finish(product(x_ref[row : row + rows, :], w), base + row, extra_refs, out_refs)
            base += x_ref.shape[0]

    return pl.pallas_call(
        kernel,
        grid=(n // width,),
        in_specs=[once(x.shape) for x in xs] + [weight_spec] + [spec for _, spec in extras],
        out_specs=tuple(spec for _, _, spec in outs),
        out_shape=tuple(jax.ShapeDtypeStruct(shape, kind) for shape, kind, _ in outs),
        compiler_params=pltpu.CompilerParams(vmem_limit_bytes=56 << 20),
        cost_estimate=FREE,
        name=name,
    )(*xs, weight, *[x for x, _ in extras])


def count_rows(xs):
    return sum(x.shape[0] for x in xs)


def project_rows(xs, weight, first, n, bias, scale, name):
    weight, layer = weight
    rows, depth = count_rows(xs), weight.shape[1]
    width = math.gcd(width_of(n, 640), first) if first else width_of(n, 640)

    def finish(result, row, extra, out):
        out[0][row : row + result.shape[0], :] = ((result + extra[0][...]) * scale).astype(BF)

    return dense(
        xs,
        (weight, pl.BlockSpec((1, depth, width), lambda i: (layer, 0, i + first // width))),
        n,
        lambda x, w: dot_on(x, w, 1, 0),
        finish,
        [((rows, n), BF, pl.BlockSpec((rows, width), lambda i: (0, i)))],
        [(bias[None, :], pl.BlockSpec((1, width), lambda i: (0, i)))],
        name,
        width,
    )[0]


def widen_rows(xs, weight, bias):
    fc_all, layer = weight
    rows, depth, n = count_rows(xs), fc_all.shape[1], fc_all.shape[2]
    width = width_of(n, 512)

    def finish(result, row, extra, out):
        active, slope = gelu_both(result + extra[0][...])
        out[0][row : row + result.shape[0], :] = active
        out[1][row : row + result.shape[0], :] = slope

    spec = pl.BlockSpec((rows, width), lambda i: (0, i))
    return dense(
        xs,
        (fc_all, pl.BlockSpec((1, depth, width), lambda i: (layer, 0, i))),
        n,
        lambda x, w: dot_on(x, w, 1, 0),
        finish,
        [((rows, n), BF, spec)] * 2,
        [(bias[None, :], pl.BlockSpec((1, width), lambda i: (0, i)))],
        "widen",
        width,
    )


def slope_rows(xs, weight, slope):
    fc_all, layer = weight
    rows, depth, n = count_rows(xs), fc_all.shape[1], fc_all.shape[2]
    width = width_of(n, 512)

    def finish(result, row, extra, out):
        grad = (result * extra[0][row : row + result.shape[0], :].astype(F32)).astype(BF)
        out[0][row : row + result.shape[0], :] = grad
        total = jnp.sum(grad.astype(F32), axis=0, keepdims=True)
        out[1][...] = total if row == 0 else out[1][...] + total

    spec = pl.BlockSpec((rows, width), lambda i: (0, i))
    return dense(
        xs,
        (fc_all, pl.BlockSpec((1, depth, width), lambda i: (layer, 0, i))),
        n,
        lambda x, w: dot_on(x, w, 1, 0),
        finish,
        [((rows, n), BF, spec), ((1, n), F32, pl.BlockSpec((1, width), lambda i: (0, i)))],
        [(slope, spec)],
        "grad_hidden",
        width,
    )


def back_rows(xs, weight, columns, name):
    weight, layer = weight
    rows = xs[0].shape[0]
    n = weight.shape[-2]
    width = width_of(n, 256)
    half = rows // 2 if lax.axis_size("tensor") == 2 else 0
    depth = weight.shape[-1]

    def kernel(*refs):
        x_refs, w_ref, out_refs = refs[: len(xs)], refs[len(xs)], refs[len(xs) + 1 :]
        w = w_ref[...].reshape(w_ref.shape[-2:])
        for row in range(0, rows, STEP):
            result = sum(
                dot_on(x_ref[row : row + STEP, :], w[:, c : c + x_ref.shape[1]], 1, 1)
                for x_ref, c in zip(x_refs, columns)
            )
            if row < half:
                out_refs[0][row : row + STEP, :] = result
            else:
                out_refs[-1][row - half : row - half + STEP, :] = result.astype(BF)

    w_spec = pl.BlockSpec((1, width, depth), lambda i: (layer, i, 0))
    kinds = [(half, F32)] if half else []
    kinds.append((rows - half, BF))
    return pl.pallas_call(
        kernel,
        grid=(n // width,),
        in_specs=[once(x.shape) for x in xs] + [w_spec],
        out_specs=tuple(pl.BlockSpec((r, width), lambda i: (0, i)) for r, _ in kinds),
        out_shape=tuple(jax.ShapeDtypeStruct((r, n), kind) for r, kind in kinds),
        compiler_params=pltpu.CompilerParams(vmem_limit_bytes=56 << 20),
        cost_estimate=FREE,
        name=name,
    )(*xs, weight)


def weight_terms(parts, n, kind, start=None, place=None, name="weight_terms"):
    depth = parts[0][1][0][0].shape[1]
    height = width_of(depth, 256)
    xs, ys = [], []
    plan = []
    for column, pairs in parts:
        for x, y, row in pairs:
            if not any(x is known for known in xs):
                xs.append(x)
            if not any(y is known for known in ys):
                ys.append(y)
        plan.append(
            (
                column,
                [
                    (
                        next(k for k, known in enumerate(xs) if known is x),
                        next(k for k, known in enumerate(ys) if known is y),
                        row,
                    )
                    for x, y, row in pairs
                ],
            )
        )
    more = []
    if start is not None:
        more.append(start)
    if place is not None and place[1] is not None:
        more.append(place[1])

    def kernel(*refs):
        x_refs, refs = refs[: len(xs)], refs[len(xs) :]
        y_refs, refs = refs[: len(ys)], refs[len(ys) :]
        out_ref = refs[-1]

        def store(a, b, value):
            if place is None:
                out_ref[:, a:b] = value.astype(kind)
            else:
                out_ref[0, :, a:b] = value.astype(kind)

        done = []
        for column, pairs in plan:
            span = y_refs[pairs[0][1]].shape[1]
            width = width_of(span, 640)
            for c in range(0, span, width):
                total = None if start is None else refs[0][:, column + c : column + c + width]
                for x, y, row in pairs:
                    count = x_refs[x].shape[0]
                    part = dot_on(x_refs[x][...], y_refs[y][row : row + count, c : c + width], 0, 0)
                    total = part if total is None else total + part
                store(column + c, column + c + width, total)
            done.append((column, column + span))
        edge = 0
        for a, b in sorted(done) + [(n, n)]:
            if a > edge:
                rest = jnp.zeros((height, a - edge), F32) if start is None else refs[0][:, edge:a]
                store(edge, a, rest)
            edge = b

    x_spec = [pl.BlockSpec((x.shape[0], height), lambda i: (0, i)) for x in xs]
    more_spec = []
    if start is not None:
        more_spec.append(pl.BlockSpec((height, n), lambda i: (i, 0)))
    aliases = {}
    if place is None:
        shape, spec = (depth, n), pl.BlockSpec((height, n), lambda i: (i, 0))
    else:
        slot = place[0]
        shape, spec = (2, depth, n), pl.BlockSpec((1, height, n), lambda i: (slot, i, 0))
        if place[1] is not None:
            more_spec.append(ANY)
            aliases = {len(xs) + len(ys) + len(more) - 1: 0}
    return pl.pallas_call(
        kernel,
        grid=(depth // height,),
        in_specs=x_spec + [once(y.shape) for y in ys] + more_spec,
        out_specs=spec,
        out_shape=jax.ShapeDtypeStruct(shape, kind),
        input_output_aliases=aliases,
        compiler_params=pltpu.CompilerParams(vmem_limit_bytes=60 << 20),
        cost_estimate=FREE,
        name=name,
    )(*xs, *ys, *more)


def over_dp(x, by, start=0, step=1):
    length = lax.axis_size("dp")
    pairs = [(i, i + by) for i in range(start, length, step) if 0 <= i + by < length]
    return lax.ppermute(x, "dp", pairs)


def near_rows(kv, swap):
    half = kv.shape[0] // 2

    def head(x):
        return lax.dynamic_slice_in_dim(x, swap * half, EDGE)

    def tail(x):
        return lax.dynamic_slice_in_dim(x, (1 - swap) * half, EDGE)

    left, right = over_dp(kv, 1), over_dp(kv, -1)
    far_left, far_right = over_dp(tail(kv), 2, 0, 2), over_dp(head(kv), -2, 1, 2)
    return (
        far_left,
        over_dp(tail(left), 1, 0, 2),
        left,
        kv,
        right,
        far_right,
        over_dp(head(right), -1, 1, 2),
    )


def to_half(whole, part, second):
    half = whole.shape[0] // 2
    zero = jnp.zeros((), F32)
    part = part.astype(F32)
    wide = jnp.concatenate((jnp.where(second == 0, part, zero), jnp.where(second == 1, part, zero)))
    return whole.astype(F32) + wide


def return_rows(grads):
    g_l2, g_l1, own, g_r1, g_r2 = grads
    return own, over_dp(g_l1, -1), over_dp(g_r1, 1), over_dp(g_l2, -2), over_dp(g_r2, 2)


def add_returned(parts, swap):
    own, from_right, from_left, for_tail, for_head = parts
    total = own.astype(F32) + from_right.astype(F32) + from_left.astype(F32)
    return to_half(to_half(total, for_tail, 1 - swap), for_head, swap).astype(BF)


def sum_everywhere(x, axis):
    length = lax.axis_size(axis)
    bit = 1
    while bit < length:
        x = x + lax.ppermute(x, axis, [(i, i ^ bit) for i in range(length)])
        bit *= 2
    return x


class Order:
    def __init__(self):
        self.last = None

    def after(self, x, *more):
        if self.last is not None:
            more += (self.last,)
        return lax.optimization_barrier((x, *more))[0] if more else x

    def done(self, x):
        self.last = x
        return x


def partner(x):
    return lax.ppermute(x, "tensor", [(0, 1), (1, 0)])


def collect(x):
    if lax.axis_size("tensor") != 2:
        return [lax.all_gather(x, "tensor", axis=0, tiled=True)]
    return [x, partner(x)]


def share(parts):
    if len(parts) == 1:
        return lax.psum_scatter(parts[0], "tensor", scatter_dimension=0, tiled=True), jnp.zeros((), BF)
    return parts[0], partner(parts[1])


def norm_parts(x):
    centred = x - jnp.mean(x, axis=-1, keepdims=True)
    scale = lax.rsqrt(jnp.mean(centred * centred, axis=-1, keepdims=True) + EPSILON)
    return centred * scale, scale


def norm_back(grad, z, scale, gain):
    e = grad * gain
    mean_e = jnp.mean(e, axis=-1, keepdims=True)
    mean_ez = jnp.mean(e * z, axis=-1, keepdims=True)
    return scale * (e - mean_e - z * mean_ez)


def gelu_both(u):
    below = 0.5 * (1.0 + lax.erf(u * math.sqrt(0.5)))
    density = jnp.exp(-0.5 * u * u) * (1.0 / math.sqrt(2.0 * math.pi))
    return (u * below).astype(BF), (below + u * density).astype(BF)


def per_device(
    frames, cotangent, segment_ids, w_qkv, w_out, w_fc1, w_fc2, bias_qv, bias_fc1, norm_vectors
):
    dp_place = lax.axis_index("dp")
    paired = lax.axis_size("tensor") == 2
    swap = lax.axis_index("tensor").astype(jnp.int32) if paired else jnp.int32(0)
    own = frames.shape[1]
    FR = own * lax.axis_size("tensor")
    half = FR // 2
    rows = 2 * EDGE + 3 * FR
    local = w_qkv.shape[2]
    heads = local // HD
    W = -(-local // 128) * 128
    fill = W - local
    vectors = norm_vectors.astype(F32)

    def widened(x):
        return jnp.pad(x, [(0, 0)] * (x.ndim - 1) + [(0, fill)]) if fill else x

    attention = jnp.concatenate(
        (widened(w_qkv).reshape(w_qkv.shape[0], 3 * W), widened(w_out)), axis=1
    )
    if attention.shape == w_fc1.shape:
        every = lax.all_gather(jnp.stack((attention, w_fc1, w_fc2)), "dp", axis=1, tiled=True)
        att, fc1, fc2 = (every, 0), (every, 1), (every, 2)
    else:
        att = lax.all_gather(attention[None], "dp", axis=1, tiled=True), 0
        every = lax.all_gather(jnp.stack((w_fc1, w_fc2)), "dp", axis=1, tiled=True)
        fc1, fc2 = (every, 0), (every, 1)
    bias_q = widened(bias_qv[0].astype(F32))
    bias_kv = jnp.concatenate((jnp.zeros((W,), F32), widened(bias_qv[1].astype(F32))))
    chosen = (jnp.arange(W)[:, None] // HD == jnp.arange(heads)[None, :]).astype(F32)
    order = Order()

    class Batch:
        pass

    batches = []
    for b in range(MB):
        m = Batch()
        batches.append(m)
        m.z1, m.r1 = norm_parts(frames[b].astype(F32))
        m.h1_own = (m.z1 * vectors[0] + vectors[1]).astype(BF)
        ids = segment_ids[b]
        reach = FR + EDGE
        padded = jnp.concatenate(
            (jnp.full((reach,), -1, jnp.int32), ids, jnp.full((reach,), 1 << 30, jnp.int32))
        )
        near = lax.dynamic_slice_in_dim(padded, dp_place * FR, rows)
        mine = jnp.concatenate(
            (
                lax.dynamic_slice_in_dim(ids, dp_place * FR + swap * half, half),
                lax.dynamic_slice_in_dim(ids, dp_place * FR + (1 - swap) * half, half),
            )
        )
        m.ranges = (
            jnp.sum((near[None, :] < mine[:, None]).astype(jnp.int32), axis=1),
            jnp.sum((near[None, :] <= mine[:, None]).astype(jnp.int32), axis=1),
        )
    m0, m1 = batches
    place = jnp.stack((swap, dp_place.astype(jnp.int32) % 2))
    for m in batches:
        m.h1 = collect(m.h1_own)

    def gated(xs, *wait):
        *rest, x = xs
        return [*rest, order.after(x, *wait)]

    def keys_values(m):
        m.kv = order.done(project_rows(gated(m.h1), att, W, 2 * W, bias_kv, 1.0, "keys_values"))

    def queries(m):
        m.q = order.done(project_rows(gated(m.h1), att, 0, W, bias_q, LOG2E * SCALE, "queries"))

    def attend(m, *wait):
        m.mixed, m.lse = attend_forward(order.after(m.q, *wait), m.pieces, m.ranges, place, heads)
        order.done(m.mixed)
        parts = back_rows([m.mixed], att, [3 * W], "attended")
        m.attended, m.attended_far = share(parts)
        order.done(parts[0])

    def second_norm(m):
        near, far = m.attended, order.after(m.attended_far)
        m.middle = frames[m.b].astype(F32) + near.astype(F32) + far.astype(F32) + vectors[4]
        m.z2, m.r2 = norm_parts(m.middle)
        h2 = order.done((m.z2 * vectors[2] + vectors[3]).astype(BF))
        m.h2 = collect(h2)

    def widen(m):
        m.active, m.slope = widen_rows(gated(m.h2), fc1, bias_fc1.astype(F32))
        order.done(m.slope)

    def grad_hidden(m):
        m.grad_u, m.grad_u_sum = slope_rows(gated(m.grad_f), fc2, m.slope)
        order.done(m.grad_u)

    def grad_normed(m):
        parts = back_rows(gated([m.grad_u]), fc1, [0], "grad_normed")
        m.grad_h2, m.grad_h2_far = share(parts)
        order.done(parts[0])

    def narrow(m):
        m.fed_parts = back_rows(gated([m.active]), fc2, [0], "narrow")
        order.done(m.fed_parts[0])

    def send_narrow(m):
        *rest, last = m.fed_parts
        m.fed, m.fed_far = share([*rest, order.after(last)])

    def grad_second_norm(m):
        m.grad_rows = cotangent[m.b].astype(F32)
        m.grad_h2 = m.grad_h2.astype(F32) + order.after(m.grad_h2_far).astype(F32)
        m.grad_middle = m.grad_rows + norm_back(m.grad_h2, m.z2, m.r2, vectors[2])
        a = order.done(m.grad_middle.astype(BF))
        m.grad_a = collect(a)

    no_bias = jnp.zeros((W,), F32)

    def attend_back(m):
        m.grad_mixed = project_rows(
            gated(m.grad_a), att, 3 * W, W, no_bias, 1.0, "grad_mixed"
        )
        delta = lax.dot_general(
            chosen,
            m.grad_mixed.astype(F32) * m.mixed.astype(F32),
            (((0,), (1,)), ((), ())),
            precision=lax.Precision.HIGHEST,
        )
        m.grad_q, *grads = attend_backward(
            m.q, m.grad_mixed, m.pieces, m.ranges, m.lse, delta, place, heads
        )
        order.done(m.grad_q)
        m.returned = return_rows(grads)

    def add_up(m, *wait):
        m.grad_kv = order.done(add_returned([order.after(x, *wait) for x in m.returned], swap))

    def grad_projected(m):
        grad_kv = order.after(m.grad_kv)
        parts = back_rows([m.grad_q, grad_kv], att, [0, W], "grad_projected")
        m.grad_h1, m.grad_h1_far = share(parts)
        order.done(parts[0])

    def rows_of(xs, y):
        pairs, row = [], 0
        for x in xs:
            pairs.append((x, y, row))
            row += x.shape[0]
        return pairs

    def finish(m):
        grad_h1 = m.grad_h1.astype(F32) + order.after(m.grad_h1_far).astype(F32)
        m.inputs_grad = m.grad_middle + norm_back(grad_h1, m.z1, m.r1, vectors[0])
        order.done(m.inputs_grad)
        m.norm_sums = jnp.stack(
            (
                jnp.sum(grad_h1 * m.z1, axis=0),
                jnp.sum(grad_h1, axis=0),
                jnp.sum(m.grad_h2 * m.z2, axis=0),
                jnp.sum(m.grad_h2, axis=0),
                jnp.sum(m.grad_middle, axis=0),
                jnp.sum(m.grad_rows, axis=0),
            )
        )

    def owned(terms, axis):
        return lax.psum_scatter(terms.astype(BF), "dp", scatter_dimension=axis, tiled=True).astype(F32)

    m0.b, m1.b = 0, 1
    keys_values(m0)
    keys_values(m1)
    queries(m0)
    queries(m1)
    m0.pieces = near_rows(m0.kv, swap)
    first_arrived = [m0.pieces[k] for k in (0, 2, 4, 5)]
    m1.pieces = near_rows(lax.optimization_barrier((m1.kv, m1.q, *first_arrived))[0], swap)
    for m in batches:
        m.grad_f = collect(lax.optimization_barrier((cotangent[m.b], m1.h1[-1]))[0])

    def term(x, y, *wait, **how):
        pairs = rows_of(gated(x, *wait), y)
        return order.done(weight_terms([(0, pairs)], w_fc1.shape[1], **how))

    attend(m0, m0.grad_f[-1], m1.grad_f[-1])
    second_norm(m0)
    attend(m1)
    widen(m0)
    grad_hidden(m0)
    grad_normed(m0)
    second_norm(m1)
    narrow(m0)
    fc2_term = term(m0.grad_f, m0.active, kind=F32)
    grad_second_norm(m0)
    fc1_term = term(m0.h2, m0.grad_u, kind=F32)
    widen(m1)
    grad_hidden(m1)
    grad_normed(m1)
    fc_terms = term(
        m1.grad_f, m1.active, m0.grad_a[-1], kind=BF, start=fc2_term, place=(1, None)
    )
    grad_second_norm(m1)
    fc_terms = term(m1.h2, m1.grad_u, kind=BF, start=fc1_term, place=(0, fc_terms))
    own_fc1, own_fc2 = owned(fc_terms, 1)
    attend_back(m0)
    send_narrow(m0)
    attend_back(m1)
    narrow(m1)
    send_narrow(m1)
    terms = weight_terms(
        [
            (0, rows_of(gated(m0.h1), m0.grad_q) + rows_of(m1.h1, m1.grad_q)),
            (3 * W, rows_of(m0.grad_a, m0.mixed) + rows_of(m1.grad_a, m1.mixed)),
        ],
        4 * W,
        F32,
    )
    order.done(terms)
    add_up(m1, m0.fed_far, m1.fed_far, *m0.returned)
    add_up(m0)
    kv_pairs = rows_of(m0.h1, m0.grad_kv) + rows_of(m1.h1, m1.grad_kv)
    terms = order.done(weight_terms([(W, kv_pairs)], 4 * W, BF, start=terms))
    own_attention = owned(lax.optimization_barrier((terms, own_fc1))[0], 0)
    grad_projected(m0)
    grad_projected(m1)
    finish(m0)
    outputs = [
        (m.middle + m.fed.astype(F32) + order.after(m.fed_far).astype(F32) + vectors[5]).astype(BF)
        for m in batches
    ]
    finish(m1)
    own_qkv = own_attention[:, : 3 * W].reshape(own_attention.shape[0], 3, W)[:, :, :local]
    own_out = own_attention[:, 3 * W :][:, :local]

    bias_parts = (
        sum(jnp.sum(m.grad_q, axis=0, dtype=F32) for m in batches)[:local],
        sum(jnp.sum(m.grad_kv[:, W:], axis=0, dtype=F32) for m in batches)[:local],
        sum(m.grad_u_sum[0] for m in batches),
    )
    norm_sums = m0.norm_sums + m1.norm_sums
    small = sum_everywhere(jnp.concatenate(bias_parts + (norm_sums.reshape(-1),)), "dp")
    bias_qv_total = small[: 2 * local].reshape(2, local)
    bias_fc1_total = small[2 * local : 2 * local + w_fc1.shape[1]]
    norm_total = sum_everywhere(small[2 * local + w_fc1.shape[1] :], "tensor").reshape(norm_sums.shape)
    return (
        jnp.stack(outputs),
        jnp.stack([m.inputs_grad for m in batches]),
        own_qkv,
        own_out,
        own_fc1,
        own_fc2,
        bias_qv_total,
        bias_fc1_total,
        norm_total,
    )


def solution(mesh):
    in_specs = (
        P(None, ("dp", "tensor"), None),
        P(None, ("dp", "tensor"), None),
        P(),
        P("dp", None, "tensor"),
        P("dp", "tensor"),
        P("dp", "tensor"),
        P("dp", "tensor"),
        P(None, "tensor"),
        P("tensor"),
        P(),
    )
    out_specs = (
        P(None, ("dp", "tensor"), None),
        P(None, ("dp", "tensor"), None),
        P("dp", None, "tensor"),
        P("dp", "tensor"),
        P("dp", "tensor"),
        P("dp", "tensor"),
        P(None, "tensor"),
        P("tensor"),
        P(),
    )
    return jax.shard_map(
        per_device, mesh=mesh, in_specs=in_specs, out_specs=out_specs, check_vma=False
    )
```

```python
import functools
import math

import jax
import jax.numpy as jnp
from jax import lax
from jax.experimental import pallas as pl
from jax.experimental.pallas import tpu as pltpu
from jax.sharding import PartitionSpec as P

HD = 80
MB = 2
EDGE = 512
EPSILON = 1e-05
NEGATIVE = -1e30
LOG2E = math.log2(math.e)
SCALE = 1.0 / math.sqrt(HD)
BF = jnp.bfloat16
F32 = jnp.float32


def head_spans(heads):
    spans = []
    for head in range(heads):
        first, last = head * HD, (head + 1) * HD
        start = first // 128 * 128
        spans.append((start, -(-last // 128) * 128 - start, first - start))
    return spans


def dot_on(a, b, a_dim, b_dim):
    return lax.dot_general(a, b, (((a_dim,), (b_dim,)), ((), ())), preferred_element_type=F32)


def in_head(rows, width, offset):
    lane = lax.broadcasted_iota(jnp.int32, (rows, width), 1)
    return (lane >= offset) & (lane < offset + HD)


def head_ones(width, offset):
    return jnp.where(in_head(1, width, offset), 1.0, 0.0).astype(BF)


def window_parts(refs, place, FR):
    swap, core = place[0], place[1]
    half = FR // 2
    left, right, last = EDGE, EDGE + 2 * FR, EDGE + 3 * FR
    inside, across = right + core * (left - right), left + core * (right - left)
    parts = []
    for ref, base in zip(refs[:3], (inside, across, EDGE + FR)):
        parts.append((ref, 0, base + swap * half, half))
        parts.append((ref, half, base + (1 - swap) * half, half))
    parts.append((refs[3], 0, core * last, EDGE))
    parts.append((refs[4], 0, (1 - core) * last, EDGE))
    return parts


def piece_parts(refs, swap, FR):
    half = FR // 2
    both = (swap * half, (1 - swap) * half)
    bases = [[base + add for add in both] for base in (EDGE, EDGE + FR, EDGE + 2 * FR)]
    bases = [[0]] + bases + [[EDGE + 3 * FR]]
    return [
        (ref, number * half, base, half)
        for ref, group in zip(refs, bases)
        for number, base in enumerate(group)
    ]


def fetch_window(refs, place, FR, window, sems):
    swap, core = place[0], place[1]
    left_direct, left_relayed, *near, right_direct, right_relayed = refs
    copies = []
    for number, (ref, row, at, rows) in enumerate(piece_parts([left_direct, *near, right_direct], swap, FR)):
        to = window.at[pl.ds(pl.multiple_of(at, EDGE), rows)]
        copies.append(pltpu.make_async_copy(ref.at[pl.ds(row, rows)], to, sems.at[number]))
        if ref is left_direct or ref is right_direct:
            other = pltpu.make_async_copy(
                left_relayed if ref is left_direct else right_relayed, to, sems.at[number]
            )
            here = core == (0 if ref is left_direct else 1)
            pl.when(here)(copies[-1].start)
            pl.when(jnp.logical_not(here))(other.start)
        else:
            copies[-1].start()
    for copy in copies:
        copy.wait()


def forward_kernel(heads, W, QB, KB, lo_ref, count_ref, place_ref, se_ref, q_ref, *refs):
    *pieces, o_ref, lse_ref, window, sems, top_s, sum_s, acc_s = refs
    fetch_window(pieces, place_ref, q_ref.shape[0], window, sems)
    spans = head_spans(heads)

    def query_block(i, carry):
        r = pl.multiple_of(i * QB, QB)
        top_s[...] = jnp.full(top_s.shape, NEGATIVE, F32)
        sum_s[...] = jnp.zeros(sum_s.shape, F32)
        acc_s[...] = jnp.zeros(acc_s.shape, F32)
        st = se_ref[0:1, pl.ds(r, QB)]
        en = se_ref[1:2, pl.ds(r, QB)]

        def chunk(c, inner):
            k0 = pl.multiple_of(lo_ref[i] + c * KB, 16)
            at = k0 + lax.broadcasted_iota(jnp.int32, (KB, QB), 0)
            mask = (at >= st) & (at < en)
            for h in range(heads):
                t, w, off = spans[h]
                q = q_ref[pl.ds(r, QB), t : t + w] * head_ones(w, off)
                v = window[pl.ds(k0, KB), W + t : W + t + w]
                s = dot_on(window[pl.ds(k0, KB), t : t + w], q, 1, 1)
                s = jnp.where(mask, s, NEGATIVE)
                before = top_s[h : h + 1, :]
                top = jnp.maximum(before, jnp.max(s, axis=0, keepdims=True))
                p = jnp.exp2(s - top)
                shrink = jnp.exp2(before - top)
                sum_s[h : h + 1, :] = sum_s[h : h + 1, :] * shrink + jnp.sum(p, axis=0, keepdims=True)
                acc_s[h, :w, :] = acc_s[h, :w, :] * shrink + dot_on(v, p.astype(BF), 0, 0)
                top_s[h : h + 1, :] = top
            return inner

        lax.fori_loop(0, count_ref[i], chunk, 0)
        for h in range(heads):
            t, w, off = spans[h]
            o = (acc_s[h, :w, :] / sum_s[h : h + 1, :]).T.astype(BF)
            o_ref[pl.ds(r, QB), t : t + w] = jnp.where(
                in_head(QB, w, off), o, o_ref[pl.ds(r, QB), t : t + w]
            )
        lse_ref[:, pl.ds(r, QB)] = top_s[...] + jnp.log2(sum_s[...])
        return carry

    lax.fori_loop(0, q_ref.shape[0] // QB, query_block, 0)


SMEM = pl.BlockSpec(memory_space=pltpu.SMEM)
VMEM = pl.BlockSpec(memory_space=pltpu.VMEM)
ANY = pl.BlockSpec(memory_space=pl.ANY)


def attend_forward(q, pieces, ranges, swap, heads, QB=256, KB=1536):
    st, en = ranges
    FR, W = q.shape
    rows = 3 * FR + 2 * EDGE
    lo, count = key_chunks(st, en, QB, KB, rows)
    return pl.pallas_call(
        functools.partial(forward_kernel, heads, W, QB, KB),
        out_shape=(
            jax.ShapeDtypeStruct((FR, W), BF),
            jax.ShapeDtypeStruct((heads, FR), F32),
        ),
        in_specs=[SMEM] * 3 + [VMEM] * 2 + [ANY] * len(pieces),
        out_specs=(VMEM, VMEM),
        scratch_shapes=[
            pltpu.VMEM((rows, 2 * W), BF),
            pltpu.SemaphoreType.DMA((8,)),
            pltpu.VMEM((heads, QB), F32),
            pltpu.VMEM((heads, QB), F32),
            pltpu.VMEM((heads, 256, QB), F32),
        ],
        compiler_params=pltpu.CompilerParams(vmem_limit_bytes=56 << 20),
        cost_estimate=pl.CostEstimate(flops=0, bytes_accessed=0, transcendentals=0),
        name="attend_forward",
    )(lo, count, swap, jnp.stack((st, en)), q, *pieces)


def backward_kernel(
    heads, W, QB, KB, lo_ref, count_ref, swap_ref, se_ref, lse_ref, delta_ref, q_ref, do_ref, *refs
):
    *refs, window, grads, dq_s, sems = refs
    number = len(refs) - 6
    pieces, dq_ref, outs = refs[:number], refs[number], refs[number + 1 :]
    fetch_window(pieces, swap_ref, q_ref.shape[0], window, sems)
    spans = head_spans(heads)
    grads[...] = jnp.zeros(grads.shape, F32)

    def query_block(i, carry):
        r = pl.multiple_of(i * QB, QB)
        dq_s[...] = jnp.zeros(dq_s.shape, F32)
        st = se_ref[0:1, pl.ds(r, QB)]
        en = se_ref[1:2, pl.ds(r, QB)]

        def chunk(c, inner):
            k0 = pl.multiple_of(lo_ref[i] + c * KB, 16)
            at = k0 + lax.broadcasted_iota(jnp.int32, (KB, QB), 0)
            mask = (at >= st) & (at < en)
            for h in range(heads):
                t, w, off = spans[h]
                ones = head_ones(w, off)
                q = q_ref[pl.ds(r, QB), t : t + w] * ones
                do = do_ref[pl.ds(r, QB), t : t + w] * ones
                k = window[pl.ds(k0, KB), t : t + w]
                v = window[pl.ds(k0, KB), W + t : W + t + w]
                s = dot_on(k, q, 1, 1)
                p = jnp.exp2(jnp.where(mask, s - lse_ref[h : h + 1, pl.ds(r, QB)], NEGATIVE))
                dp = dot_on(v, do, 1, 1)
                ds = (p * (dp - delta_ref[h : h + 1, pl.ds(r, QB)])).astype(BF)
                grads[pl.ds(k0, KB), W + t : W + t + w] += dot_on(p.astype(BF), do, 1, 0)
                grads[pl.ds(k0, KB), t : t + w] += dot_on(ds, q, 1, 0)
                dq_s[h, :, :w] += dot_on(ds, k, 0, 0)
            return inner

        lax.fori_loop(0, count_ref[i], chunk, 0)
        for h in range(heads):
            t, w, off = spans[h]
            dq = (dq_s[h, :, :w] * SCALE).astype(BF)
            dq_ref[pl.ds(r, QB), t : t + w] = jnp.where(
                in_head(QB, w, off), dq, dq_ref[pl.ds(r, QB), t : t + w]
            )
        return carry

    lax.fori_loop(0, q_ref.shape[0] // QB, query_block, 0)
    for ref, row, at, rows in window_parts(outs, swap_ref, q_ref.shape[0]):

        def store(j, carry, ref=ref, row=row, at=at):
            to = pl.multiple_of(row + j * 128, 128)
            here = pl.multiple_of(at + j * 128, 128)
            ref[pl.ds(to, 128), :W] = (grads[pl.ds(here, 128), :W] * math.log(2.0)).astype(BF)
            ref[pl.ds(to, 128), W:] = grads[pl.ds(here, 128), W:].astype(BF)
            return carry

        lax.fori_loop(0, rows // 128, store, 0)


def attend_backward(q, do, pieces, ranges, lse, delta, swap, heads, QB=256, KB=768):
    st, en = ranges
    FR, W = q.shape
    rows = 3 * FR + 2 * EDGE
    lo, count = key_chunks(st, en, QB, KB, rows)
    grads = [(piece, 2 * W) for piece in (FR, FR, FR, EDGE, EDGE)]
    return pl.pallas_call(
        functools.partial(backward_kernel, heads, W, QB, KB),
        out_shape=(jax.ShapeDtypeStruct((FR, W), BF),)
        + tuple(jax.ShapeDtypeStruct(shape, BF) for shape in grads),
        in_specs=[SMEM] * 3 + [VMEM] * 5 + [ANY] * len(pieces),
        out_specs=(VMEM,) * (1 + len(grads)),
        scratch_shapes=[
            pltpu.VMEM((rows, 2 * W), BF),
            pltpu.VMEM((rows, 2 * W), F32),
            pltpu.VMEM((heads, QB, 256), F32),
            pltpu.SemaphoreType.DMA((8,)),
        ],
        compiler_params=pltpu.CompilerParams(vmem_limit_bytes=60 << 20),
        cost_estimate=pl.CostEstimate(flops=0, bytes_accessed=0, transcendentals=0),
        name="attend_backward",
    )(lo, count, swap, jnp.stack((st, en)), lse, delta, q, do, *pieces)


def key_chunks(st, en, QB, KB, rows):
    lo = st[::QB] // 16 * 16
    count = (en[QB - 1 :: QB] - lo + KB - 1) // KB
    return jnp.minimum(lo, rows - count * KB), count


STEP = 256
FREE = pl.CostEstimate(flops=0, bytes_accessed=0, transcendentals=0)


def once(shape):
    return pl.BlockSpec(shape, lambda i: (0,) * len(shape), pipeline_mode=pl.Buffered(1))


def width_of(n, limit):
    return max(w for w in range(128, min(n, limit) + 1, 128) if n % w == 0)


def dense(xs, weights, n, product, finish, outs, extras=(), name="dense", width=512):
    weight, weight_spec = weights

    def kernel(*refs):
        x_refs, refs = refs[: len(xs)], refs[len(xs) :]
        w_ref, refs = refs[0], refs[1:]
        extra_refs, out_refs = refs[: len(extras)], refs[len(extras) :]
        w = w_ref[...].reshape(w_ref.shape[-2:])
        base = 0
        for x_ref in x_refs:
            for row in range(0, x_ref.shape[0], STEP):
                rows = min(STEP, x_ref.shape[0] - row)
                finish(product(x_ref[row : row + rows, :], w), base + row, extra_refs, out_refs)
            base += x_ref.shape[0]

    return pl.pallas_call(
        kernel,
        grid=(n // width,),
        in_specs=[once(x.shape) for x in xs] + [weight_spec] + [spec for _, spec in extras],
        out_specs=tuple(spec for _, _, spec in outs),
        out_shape=tuple(jax.ShapeDtypeStruct(shape, kind) for shape, kind, _ in outs),
        compiler_params=pltpu.CompilerParams(vmem_limit_bytes=26 << 20),
        cost_estimate=FREE,
        name=name,
    )(*xs, weight, *[x for x, _ in extras])


def count_rows(xs):
    return sum(x.shape[0] for x in xs)


def project_rows(xs, weight, first, n, bias, scale, name):
    weight, layer = weight
    rows, depth = count_rows(xs), weight.shape[1]
    width = math.gcd(width_of(n, 640), first) if first else width_of(n, 640)

    def finish(result, row, extra, out):
        out[0][row : row + result.shape[0], :] = ((result + extra[0][...]) * scale).astype(BF)

    return dense(
        xs,
        (weight, pl.BlockSpec((1, depth, width), lambda i: (layer, 0, i + first // width))),
        n,
        lambda x, w: dot_on(x, w, 1, 0),
        finish,
        [((rows, n), BF, pl.BlockSpec((rows, width), lambda i: (0, i)))],
        [(bias[None, :], pl.BlockSpec((1, width), lambda i: (0, i)))],
        name,
        width,
    )[0]


def widen_rows(xs, weight, bias):
    fc_all, layer = weight
    rows, depth, n = count_rows(xs), fc_all.shape[1], fc_all.shape[2]
    width = width_of(n, 512)

    def finish(result, row, extra, out):
        active, slope = gelu_both(result + extra[0][...])
        out[0][row : row + result.shape[0], :] = active
        out[1][row : row + result.shape[0], :] = slope

    spec = pl.BlockSpec((rows, width), lambda i: (0, i))
    return dense(
        xs,
        (fc_all, pl.BlockSpec((1, depth, width), lambda i: (layer, 0, i))),
        n,
        lambda x, w: dot_on(x, w, 1, 0),
        finish,
        [((rows, n), BF, spec)] * 2,
        [(bias[None, :], pl.BlockSpec((1, width), lambda i: (0, i)))],
        "widen",
        width,
    )


def slope_rows(xs, weight, slope):
    fc_all, layer = weight
    rows, depth, n = count_rows(xs), fc_all.shape[1], fc_all.shape[2]
    width = width_of(n, 512)

    def finish(result, row, extra, out):
        grad = (result * extra[0][row : row + result.shape[0], :].astype(F32)).astype(BF)
        out[0][row : row + result.shape[0], :] = grad
        total = jnp.sum(grad.astype(F32), axis=0, keepdims=True)
        out[1][...] = total if row == 0 else out[1][...] + total

    spec = pl.BlockSpec((rows, width), lambda i: (0, i))
    return dense(
        xs,
        (fc_all, pl.BlockSpec((1, depth, width), lambda i: (layer, 0, i))),
        n,
        lambda x, w: dot_on(x, w, 1, 0),
        finish,
        [((rows, n), BF, spec), ((1, n), F32, pl.BlockSpec((1, width), lambda i: (0, i)))],
        [(slope, spec)],
        "grad_hidden",
        width,
    )


def back_rows(xs, weight, columns, name):
    weight, layer = weight
    rows = xs[0].shape[0]
    n = weight.shape[-2]
    width = width_of(n, 256)
    half = rows // 2 if lax.axis_size("tensor") == 2 else 0
    depth = weight.shape[-1]

    def kernel(*refs):
        x_refs, w_ref, out_refs = refs[: len(xs)], refs[len(xs)], refs[len(xs) + 1 :]
        w = w_ref[...].reshape(w_ref.shape[-2:])
        for row in range(0, rows, STEP):
            result = sum(
                dot_on(x_ref[row : row + STEP, :], w[:, c : c + x_ref.shape[1]], 1, 1)
                for x_ref, c in zip(x_refs, columns)
            )
            if row < half:
                out_refs[0][row : row + STEP, :] = result
            else:
                out_refs[-1][row - half : row - half + STEP, :] = result.astype(BF)

    w_spec = pl.BlockSpec((1, width, depth), lambda i: (layer, i, 0))
    kinds = [(half, F32)] if half else []
    kinds.append((rows - half, BF))
    return pl.pallas_call(
        kernel,
        grid=(n // width,),
        in_specs=[once(x.shape) for x in xs] + [w_spec],
        out_specs=tuple(pl.BlockSpec((r, width), lambda i: (0, i)) for r, _ in kinds),
        out_shape=tuple(jax.ShapeDtypeStruct((r, n), kind) for r, kind in kinds),
        compiler_params=pltpu.CompilerParams(vmem_limit_bytes=26 << 20),
        cost_estimate=FREE,
        name=name,
    )(*xs, weight)


def weight_terms(parts, n, kind, start=None, place=None, room=26):
    depth = parts[0][1][0][0].shape[1]
    height = width_of(depth, 256)
    xs, ys = [], []
    plan = []
    for column, pairs in parts:
        for x, y, row in pairs:
            if not any(x is known for known in xs):
                xs.append(x)
            if not any(y is known for known in ys):
                ys.append(y)
        plan.append(
            (
                column,
                [
                    (
                        next(k for k, known in enumerate(xs) if known is x),
                        next(k for k, known in enumerate(ys) if known is y),
                        row,
                    )
                    for x, y, row in pairs
                ],
            )
        )
    more = []
    if start is not None:
        more.append(start)
    if place is not None and place[1] is not None:
        more.append(place[1])

    def kernel(*refs):
        x_refs, refs = refs[: len(xs)], refs[len(xs) :]
        y_refs, refs = refs[: len(ys)], refs[len(ys) :]
        out_ref = refs[-1]

        def store(a, b, value):
            if place is None:
                out_ref[:, a:b] = value.astype(kind)
            else:
                out_ref[0, :, a:b] = value.astype(kind)

        done = []
        for column, pairs in plan:
            span = y_refs[pairs[0][1]].shape[1]
            width = width_of(span, 640)
            for c in range(0, span, width):
                total = None if start is None else refs[0][:, column + c : column + c + width]
                for x, y, row in pairs:
                    count = x_refs[x].shape[0]
                    part = dot_on(x_refs[x][...], y_refs[y][row : row + count, c : c + width], 0, 0)
                    total = part if total is None else total + part
                store(column + c, column + c + width, total)
            done.append((column, column + span))
        edge = 0
        for a, b in sorted(done) + [(n, n)]:
            if a > edge:
                rest = jnp.zeros((height, a - edge), F32) if start is None else refs[0][:, edge:a]
                store(edge, a, rest)
            edge = b

    x_spec = [pl.BlockSpec((x.shape[0], height), lambda i: (0, i)) for x in xs]
    more_spec = []
    if start is not None:
        more_spec.append(pl.BlockSpec((height, n), lambda i: (i, 0)))
    aliases = {}
    if place is None:
        shape, spec = (depth, n), pl.BlockSpec((height, n), lambda i: (i, 0))
    else:
        slot = place[0]
        shape, spec = (2, depth, n), pl.BlockSpec((1, height, n), lambda i: (slot, i, 0))
        if place[1] is not None:
            more_spec.append(ANY)
            aliases = {len(xs) + len(ys) + len(more) - 1: 0}
    return pl.pallas_call(
        kernel,
        grid=(depth // height,),
        in_specs=x_spec + [once(y.shape) for y in ys] + more_spec,
        out_specs=spec,
        out_shape=jax.ShapeDtypeStruct(shape, kind),
        input_output_aliases=aliases,
        compiler_params=pltpu.CompilerParams(vmem_limit_bytes=room << 20),
        cost_estimate=FREE,
        name="weight_terms",
    )(*xs, *ys, *more)


def across(x):
    length = lax.axis_size("dp")
    pairs = [(i, i - 1 + 2 * (i % 2)) for i in range(length)]
    return lax.ppermute(x, "dp", [(i, j) for i, j in pairs if 0 <= j < length])


def inside(x):
    return lax.ppermute(x, "dp", [(i, i ^ 1) for i in range(lax.axis_size("dp"))])


def over_dp(x, by, start=0, step=1):
    length = lax.axis_size("dp")
    pairs = [(i, i + by) for i in range(start, length, step) if 0 <= i + by < length]
    return lax.ppermute(x, "dp", pairs)


def near_rows(kv, swap):
    half = kv.shape[0] // 2

    def head(x):
        return lax.dynamic_slice_in_dim(x, swap * half, EDGE)

    def tail(x):
        return lax.dynamic_slice_in_dim(x, (1 - swap) * half, EDGE)

    left, right = over_dp(kv, 1), over_dp(kv, -1)
    far_left, far_right = over_dp(tail(kv), 2, 0, 2), over_dp(head(kv), -2, 1, 2)
    return (
        far_left,
        over_dp(tail(left), 1, 0, 2),
        left,
        kv,
        right,
        far_right,
        over_dp(head(right), -1, 1, 2),
    )


BLOCK = 256


def add_far(near, far, second):
    rows, width = far.shape
    steps = rows // BLOCK

    def kernel(second_ref, near_ref, far_ref, out_ref):
        out_ref[...] = (near_ref[...].astype(F32) + far_ref[...].astype(F32)).astype(BF)

    here = pl.BlockSpec((BLOCK, width), lambda i, s: (s[0] * steps + i, 0))
    return pl.pallas_call(
        kernel,
        grid_spec=pltpu.PrefetchScalarGridSpec(
            num_scalar_prefetch=1,
            grid=(steps,),
            in_specs=[here, pl.BlockSpec((BLOCK, width), lambda i, s: (i, 0))],
            out_specs=here,
        ),
        out_shape=jax.ShapeDtypeStruct(near.shape, BF),
        input_output_aliases={1: 0},
        cost_estimate=FREE,
        name="add_far",
    )(second[None], near, far)


def return_rows(grads, place):
    swap, core = place[0], place[1]
    near_inside, near_across, own, far_across, far_inside = grads
    head, tail = swap, 1 - swap
    near_across = add_far(near_across, inside(far_inside), jnp.where(core == 0, tail, head))
    from_across = across(near_across)
    near_inside = add_far(near_inside, across(far_across), jnp.where(core == 0, head, tail))
    return (own, from_across, inside(near_inside)), near_across


def add_returned(parts):
    rows, width = parts[0].shape

    def kernel(*refs):
        refs[-1][...] = sum(ref[...].astype(F32) for ref in refs[:-1]).astype(BF)

    block = pl.BlockSpec((BLOCK, width), lambda i: (i, 0))
    return pl.pallas_call(
        kernel,
        grid=(rows // BLOCK,),
        in_specs=[block] * len(parts),
        out_specs=block,
        out_shape=jax.ShapeDtypeStruct((rows, width), BF),
        cost_estimate=FREE,
        name="add_returned",
    )(*parts)


def sum_everywhere(x, axis):
    length = lax.axis_size(axis)
    bit = 1
    while bit < length:
        x = x + lax.ppermute(x, axis, [(i, i ^ bit) for i in range(length)])
        bit *= 2
    return x


class Order:
    def __init__(self):
        self.last = None

    def after(self, x, *more):
        if self.last is not None:
            more += (self.last,)
        return lax.optimization_barrier((x, *more))[0] if more else x

    def done(self, x):
        self.last = x
        return x


def partner(x):
    return lax.ppermute(x, "tensor", [(0, 1), (1, 0)])


def collect(x):
    if lax.axis_size("tensor") != 2:
        return [lax.all_gather(x, "tensor", axis=0, tiled=True)]
    return [x, partner(x)]


def share(parts):
    if len(parts) == 1:
        return lax.psum_scatter(parts[0], "tensor", scatter_dimension=0, tiled=True), jnp.zeros((), BF)
    return parts[0], partner(parts[1])


def norm_parts(x):
    centred = x - jnp.mean(x, axis=-1, keepdims=True)
    scale = lax.rsqrt(jnp.mean(centred * centred, axis=-1, keepdims=True) + EPSILON)
    return centred * scale, scale


def norm_back(grad, z, scale, gain):
    e = grad * gain
    mean_e = jnp.mean(e, axis=-1, keepdims=True)
    mean_ez = jnp.mean(e * z, axis=-1, keepdims=True)
    return scale * (e - mean_e - z * mean_ez)


def gelu_both(u):
    below = 0.5 * (1.0 + lax.erf(u * math.sqrt(0.5)))
    density = jnp.exp(-0.5 * u * u) * (1.0 / math.sqrt(2.0 * math.pi))
    return (u * below).astype(BF), (below + u * density).astype(BF)


def per_device(
    frames, cotangent, segment_ids, w_qkv, w_out, w_fc1, w_fc2, bias_qv, bias_fc1, norm_vectors
):
    dp_place = lax.axis_index("dp")
    paired = lax.axis_size("tensor") == 2
    swap = lax.axis_index("tensor").astype(jnp.int32) if paired else jnp.int32(0)
    own = frames.shape[1]
    FR = own * lax.axis_size("tensor")
    half = FR // 2
    rows = 2 * EDGE + 3 * FR
    local = w_qkv.shape[2]
    heads = local // HD
    W = -(-local // 128) * 128
    fill = W - local
    vectors = norm_vectors.astype(F32)

    def widened(x):
        return jnp.pad(x, [(0, 0)] * (x.ndim - 1) + [(0, fill)]) if fill else x

    attention = jnp.concatenate(
        (widened(w_qkv).reshape(w_qkv.shape[0], 3 * W), widened(w_out)), axis=1
    )
    att = lax.all_gather(attention[None], "dp", axis=1, tiled=True), 0
    bias_q = widened(bias_qv[0].astype(F32))
    bias_kv = jnp.concatenate((jnp.zeros((W,), F32), widened(bias_qv[1].astype(F32))))
    chosen = (jnp.arange(W)[:, None] // HD == jnp.arange(heads)[None, :]).astype(F32)
    order = Order()

    class Batch:
        pass

    batches = []
    for b in range(MB):
        m = Batch()
        batches.append(m)
        m.z1, m.r1 = norm_parts(frames[b].astype(F32))
        m.h1_own = (m.z1 * vectors[0] + vectors[1]).astype(BF)
        ids = segment_ids[b]
        reach = FR + EDGE
        padded = jnp.concatenate(
            (jnp.full((reach,), -1, jnp.int32), ids, jnp.full((reach,), 1 << 30, jnp.int32))
        )
        near = lax.dynamic_slice_in_dim(padded, dp_place * FR, rows)
        mine = jnp.concatenate(
            (
                lax.dynamic_slice_in_dim(ids, dp_place * FR + swap * half, half),
                lax.dynamic_slice_in_dim(ids, dp_place * FR + (1 - swap) * half, half),
            )
        )
        m.ranges = (
            jnp.sum((near[None, :] < mine[:, None]).astype(jnp.int32), axis=1),
            jnp.sum((near[None, :] <= mine[:, None]).astype(jnp.int32), axis=1),
        )
    m0, m1 = batches
    place = jnp.stack((swap, dp_place.astype(jnp.int32) % 2))
    for m in batches:
        m.h1 = collect(m.h1_own)

    def gated(xs, *wait):
        *rest, x = xs
        return [*rest, order.after(x, *wait)]

    def keys_values(m, *wait):
        m.kv = order.done(project_rows(gated(m.h1, *wait), att, W, 2 * W, bias_kv, 1.0, "keys_values"))

    def queries(m):
        m.q = order.done(project_rows(gated(m.h1), att, 0, W, bias_q, LOG2E * SCALE, "queries"))

    def attend(m, *wait):
        m.mixed, m.lse = attend_forward(order.after(m.q, *wait), m.pieces, m.ranges, place, heads)
        order.done(m.mixed)
        parts = back_rows([m.mixed], att, [3 * W], "attended")
        m.attended, m.attended_far = share(parts)
        order.done(parts[0])

    def second_norm(m):
        near, far = m.attended, order.after(m.attended_far)
        m.middle = frames[m.b].astype(F32) + near.astype(F32) + far.astype(F32) + vectors[4]
        m.z2, m.r2 = norm_parts(m.middle)
        h2 = order.done((m.z2 * vectors[2] + vectors[3]).astype(BF))
        m.h2 = collect(h2)

    def widen(m):
        m.active, m.slope = widen_rows(gated(m.h2), fc1, bias_fc1.astype(F32))
        order.done(m.slope)

    def grad_hidden(m):
        m.grad_u, m.grad_u_sum = slope_rows(gated(m.grad_f), fc2, m.slope)
        order.done(m.grad_u)

    def grad_normed(m):
        parts = back_rows(gated([m.grad_u]), fc1, [0], "grad_normed")
        m.grad_h2, m.grad_h2_far = share(parts)
        order.done(parts[0])

    def narrow(m, *wait):
        m.fed_parts = back_rows(gated([m.active], *wait), fc2, [0], "narrow")
        order.done(m.fed_parts[0])

    def send_narrow(m):
        *rest, last = m.fed_parts
        m.fed, m.fed_far = share([*rest, order.after(last)])

    def grad_second_norm(m):
        m.grad_rows = cotangent[m.b].astype(F32)
        m.grad_h2 = m.grad_h2.astype(F32) + order.after(m.grad_h2_far).astype(F32)
        m.grad_middle = m.grad_rows + norm_back(m.grad_h2, m.z2, m.r2, vectors[2])
        a = order.done(m.grad_middle.astype(BF))
        m.grad_a = collect(a)

    no_bias = jnp.zeros((W,), F32)

    def attend_back(m, *wait):
        m.grad_mixed = project_rows(
            gated(m.grad_a), att, 3 * W, W, no_bias, 1.0, "grad_mixed"
        )
        delta = lax.dot_general(
            chosen,
            m.grad_mixed.astype(F32) * m.mixed.astype(F32),
            (((0,), (1,)), ((), ())),
            precision=lax.Precision.HIGHEST,
        )
        m.grad_q, *grads = attend_backward(
            lax.optimization_barrier((m.q, *wait))[0], m.grad_mixed, m.pieces, m.ranges, m.lse, delta, place, heads
        )
        order.done(m.grad_q)
        m.returned, m.ready = return_rows(grads, place)

    def add_up(m, *wait):
        m.grad_kv = order.done(add_returned([order.after(x, *wait) for x in m.returned]))

    def grad_projected(m):
        grad_kv = order.after(m.grad_kv)
        parts = back_rows([m.grad_q, grad_kv], att, [0, W], "grad_projected")
        m.grad_h1, m.grad_h1_far = share(parts)
        order.done(parts[0])

    def rows_of(xs, y):
        pairs, row = [], 0
        for x in xs:
            pairs.append((x, y, row))
            row += x.shape[0]
        return pairs

    def finish(m):
        grad_h1 = m.grad_h1.astype(F32) + order.after(m.grad_h1_far).astype(F32)
        m.inputs_grad = m.grad_middle + norm_back(grad_h1, m.z1, m.r1, vectors[0])
        order.done(m.inputs_grad)
        m.norm_sums = jnp.stack(
            (
                jnp.sum(grad_h1 * m.z1, axis=0),
                jnp.sum(grad_h1, axis=0),
                jnp.sum(m.grad_h2 * m.z2, axis=0),
                jnp.sum(m.grad_h2, axis=0),
                jnp.sum(m.grad_middle, axis=0),
                jnp.sum(m.grad_rows, axis=0),
            )
        )

    def owned(terms, axis):
        return lax.psum_scatter(terms.astype(BF), "dp", scatter_dimension=axis, tiled=True).astype(F32)

    m0.b, m1.b = 0, 1
    keys_values(m0, m1.h1[-1])
    keys_values(m1)
    queries(m0)
    queries(m1)
    m0.pieces = near_rows(m0.kv, swap)
    first_arrived = [m0.pieces[k] for k in (0, 2, 4, 5)]
    w_fc = lax.optimization_barrier((jnp.stack((w_fc1, w_fc2)), *first_arrived))[0]
    fc_all = lax.all_gather(w_fc, "dp", axis=1, tiled=True)
    fc1, fc2 = (fc_all, 0), (fc_all, 1)
    m1.pieces = near_rows(lax.optimization_barrier((m1.kv, m1.q, *first_arrived))[0], swap)
    for m in batches:
        m.grad_f = collect(lax.optimization_barrier((cotangent[m.b], m1.h1[-1]))[0])

    def term(x, y, *wait, **how):
        pairs = rows_of(gated(x, *wait), y)
        return order.done(weight_terms([(0, pairs)], w_fc1.shape[1], **how))

    attend(m0, m0.grad_f[-1], m1.grad_f[-1])
    second_norm(m0)
    attend(m1)
    widen(m0)
    grad_hidden(m0)
    grad_normed(m0)
    second_norm(m1)
    narrow(m0)
    fc2_term = term(m0.grad_f, m0.active, kind=F32)
    grad_second_norm(m0)
    fc1_term = term(m0.h2, m0.grad_u, kind=F32)
    widen(m1)
    grad_hidden(m1)
    grad_normed(m1)
    fc_terms = term(
        m1.grad_f, m1.active, m0.grad_a[-1], kind=BF, start=fc2_term, place=(1, None)
    )
    grad_second_norm(m1)
    fc_terms = term(m1.h2, m1.grad_u, kind=BF, start=fc1_term, place=(0, fc_terms))
    own_fc1, own_fc2 = owned(fc_terms, 1)
    attend_back(m0, m1.grad_a[-1])
    send_narrow(m0)
    attend_back(m1, m0.ready)
    narrow(m1, m0.fed_far)
    send_narrow(m1)
    terms = weight_terms(
        [
            (0, rows_of(gated(m0.h1, m1.ready), m0.grad_q) + rows_of(m1.h1, m1.grad_q)),
            (3 * W, rows_of(m0.grad_a, m0.mixed) + rows_of(m1.grad_a, m1.mixed)),
        ],
        4 * W,
        F32,
    )
    order.done(terms)
    add_up(m0)
    grad_projected(m0)
    add_up(m1, m1.fed_far)
    kv_pairs = rows_of(m0.h1, m0.grad_kv) + rows_of(gated(m1.h1), m1.grad_kv)
    terms = order.done(weight_terms([(W, kv_pairs)], 4 * W, BF, start=terms))
    grad_projected(m1)
    own_attention = owned(lax.optimization_barrier((terms, own_fc1))[0], 0)
    finish(m0)
    outputs = [
        (m.middle + m.fed.astype(F32) + order.after(m.fed_far).astype(F32) + vectors[5]).astype(BF)
        for m in batches
    ]
    finish(m1)
    own_qkv = own_attention[:, : 3 * W].reshape(own_attention.shape[0], 3, W)[:, :, :local]
    own_out = own_attention[:, 3 * W :][:, :local]

    bias_parts = (
        sum(jnp.sum(m.grad_q, axis=0, dtype=F32) for m in batches)[:local],
        sum(jnp.sum(m.grad_kv[:, W:], axis=0, dtype=F32) for m in batches)[:local],
        sum(m.grad_u_sum[0] for m in batches),
    )
    norm_sums = m0.norm_sums + m1.norm_sums
    small = sum_everywhere(jnp.concatenate(bias_parts + (norm_sums.reshape(-1),)), "dp")
    bias_qv_total = small[: 2 * local].reshape(2, local)
    bias_fc1_total = small[2 * local : 2 * local + w_fc1.shape[1]]
    norm_total = sum_everywhere(small[2 * local + w_fc1.shape[1] :], "tensor").reshape(norm_sums.shape)
    return (
        jnp.stack(outputs),
        jnp.stack([m.inputs_grad for m in batches]),
        own_qkv,
        own_out,
        own_fc1,
        own_fc2,
        bias_qv_total,
        bias_fc1_total,
        norm_total,
    )


def solution(mesh):
    in_specs = (
        P(None, ("dp", "tensor"), None),
        P(None, ("dp", "tensor"), None),
        P(),
        P("dp", None, "tensor"),
        P("dp", "tensor"),
        P("dp", "tensor"),
        P("dp", "tensor"),
        P(None, "tensor"),
        P("tensor"),
        P(),
    )
    out_specs = (
        P(None, ("dp", "tensor"), None),
        P(None, ("dp", "tensor"), None),
        P("dp", None, "tensor"),
        P("dp", "tensor"),
        P("dp", "tensor"),
        P("dp", "tensor"),
        P(None, "tensor"),
        P("tensor"),
        P(),
    )
    return jax.shard_map(
        per_device, mesh=mesh, in_specs=in_specs, out_specs=out_specs, check_vma=False
    )
```

```python
import functools
import math

import jax
import jax.numpy as jnp
from jax import lax
from jax.experimental import pallas as pl
from jax.experimental.pallas import tpu as pltpu
from jax.sharding import PartitionSpec as P

HD = 80
MB = 2
EDGE = 512
EPSILON = 1e-05
NEGATIVE = -1e30
LOG2E = math.log2(math.e)
SCALE = 1.0 / math.sqrt(HD)
BF = jnp.bfloat16
F32 = jnp.float32


def head_spans(heads):
    spans = []
    for head in range(heads):
        first, last = head * HD, (head + 1) * HD
        start = first // 128 * 128
        spans.append((start, -(-last // 128) * 128 - start, first - start))
    return spans


def dot_on(a, b, a_dim, b_dim):
    return lax.dot_general(a, b, (((a_dim,), (b_dim,)), ((), ())), preferred_element_type=F32)


def in_head(rows, width, offset):
    lane = lax.broadcasted_iota(jnp.int32, (rows, width), 1)
    return (lane >= offset) & (lane < offset + HD)


def head_ones(width, offset):
    return jnp.where(in_head(1, width, offset), 1.0, 0.0).astype(BF)


def window_parts(refs, place, FR):
    swap, core = place[0], place[1]
    half = FR // 2
    left, right, last = EDGE, EDGE + 2 * FR, EDGE + 3 * FR
    inside, across = right + core * (left - right), left + core * (right - left)
    parts = []
    for ref, base in zip(refs[:3], (inside, across, EDGE + FR)):
        parts.append((ref, 0, base + swap * half, half))
        parts.append((ref, half, base + (1 - swap) * half, half))
    parts.append((refs[3], 0, core * last, EDGE))
    parts.append((refs[4], 0, (1 - core) * last, EDGE))
    return parts


def piece_parts(refs, swap, FR):
    half = FR // 2
    both = (swap * half, (1 - swap) * half)
    bases = [[base + add for add in both] for base in (EDGE, EDGE + FR, EDGE + 2 * FR)]
    bases = [[0]] + bases + [[EDGE + 3 * FR]]
    return [
        (ref, number * half, base, half)
        for ref, group in zip(refs, bases)
        for number, base in enumerate(group)
    ]


def fetch_window(refs, place, FR, window, sems):
    swap, core = place[0], place[1]
    left_direct, left_relayed, *near, right_direct, right_relayed = refs
    copies = []
    for number, (ref, row, at, rows) in enumerate(piece_parts([left_direct, *near, right_direct], swap, FR)):
        to = window.at[pl.ds(pl.multiple_of(at, EDGE), rows)]
        copies.append(pltpu.make_async_copy(ref.at[pl.ds(row, rows)], to, sems.at[number]))
        if ref is left_direct or ref is right_direct:
            other = pltpu.make_async_copy(
                left_relayed if ref is left_direct else right_relayed, to, sems.at[number]
            )
            here = core == (0 if ref is left_direct else 1)
            pl.when(here)(copies[-1].start)
            pl.when(jnp.logical_not(here))(other.start)
        else:
            copies[-1].start()
    for copy in copies:
        copy.wait()


def forward_kernel(heads, W, QB, KB, lo_ref, count_ref, place_ref, se_ref, q_ref, *refs):
    *pieces, o_ref, lse_ref, window, sems, top_s, sum_s, acc_s = refs
    fetch_window(pieces, place_ref, q_ref.shape[0], window, sems)
    spans = head_spans(heads)

    def query_block(i, carry):
        r = pl.multiple_of(i * QB, QB)
        top_s[...] = jnp.full(top_s.shape, NEGATIVE, F32)
        sum_s[...] = jnp.zeros(sum_s.shape, F32)
        acc_s[...] = jnp.zeros(acc_s.shape, F32)
        st = se_ref[0:1, pl.ds(r, QB)]
        en = se_ref[1:2, pl.ds(r, QB)]

        def chunk(c, inner):
            k0 = pl.multiple_of(lo_ref[i] + c * KB, 16)
            at = k0 + lax.broadcasted_iota(jnp.int32, (KB, QB), 0)
            mask = (at >= st) & (at < en)
            for h in range(heads):
                t, w, off = spans[h]
                q = q_ref[pl.ds(r, QB), t : t + w] * head_ones(w, off)
                v = window[pl.ds(k0, KB), W + t : W + t + w]
                s = dot_on(window[pl.ds(k0, KB), t : t + w], q, 1, 1)
                s = jnp.where(mask, s, NEGATIVE)
                before = top_s[h : h + 1, :]
                top = jnp.maximum(before, jnp.max(s, axis=0, keepdims=True))
                p = jnp.exp2(s - top)
                shrink = jnp.exp2(before - top)
                sum_s[h : h + 1, :] = sum_s[h : h + 1, :] * shrink + jnp.sum(p, axis=0, keepdims=True)
                acc_s[h, :w, :] = acc_s[h, :w, :] * shrink + dot_on(v, p.astype(BF), 0, 0)
                top_s[h : h + 1, :] = top
            return inner

        lax.fori_loop(0, count_ref[i], chunk, 0)
        for h in range(heads):
            t, w, off = spans[h]
            o = (acc_s[h, :w, :] / sum_s[h : h + 1, :]).T.astype(BF)
            o_ref[pl.ds(r, QB), t : t + w] = jnp.where(
                in_head(QB, w, off), o, o_ref[pl.ds(r, QB), t : t + w]
            )
        lse_ref[:, pl.ds(r, QB)] = top_s[...] + jnp.log2(sum_s[...])
        return carry

    lax.fori_loop(0, q_ref.shape[0] // QB, query_block, 0)


SMEM = pl.BlockSpec(memory_space=pltpu.SMEM)
VMEM = pl.BlockSpec(memory_space=pltpu.VMEM)
ANY = pl.BlockSpec(memory_space=pl.ANY)


def attend_forward(q, pieces, ranges, swap, heads, QB=256, KB=1536):
    st, en = ranges
    FR, W = q.shape
    rows = 3 * FR + 2 * EDGE
    lo, count = key_chunks(st, en, QB, KB, rows)
    return pl.pallas_call(
        functools.partial(forward_kernel, heads, W, QB, KB),
        out_shape=(
            jax.ShapeDtypeStruct((FR, W), BF),
            jax.ShapeDtypeStruct((heads, FR), F32),
        ),
        in_specs=[SMEM] * 3 + [VMEM] * 2 + [ANY] * len(pieces),
        out_specs=(VMEM, VMEM),
        scratch_shapes=[
            pltpu.VMEM((rows, 2 * W), BF),
            pltpu.SemaphoreType.DMA((8,)),
            pltpu.VMEM((heads, QB), F32),
            pltpu.VMEM((heads, QB), F32),
            pltpu.VMEM((heads, 256, QB), F32),
        ],
        compiler_params=pltpu.CompilerParams(vmem_limit_bytes=56 << 20),
        cost_estimate=pl.CostEstimate(flops=0, bytes_accessed=0, transcendentals=0),
        name="attend_forward",
    )(lo, count, swap, jnp.stack((st, en)), q, *pieces)


def backward_kernel(
    heads, W, QB, KB, lo_ref, count_ref, swap_ref, se_ref, lse_ref, delta_ref, q_ref, do_ref, *refs
):
    *refs, window, grads, dq_s, sems = refs
    number = len(refs) - 6
    pieces, dq_ref, outs = refs[:number], refs[number], refs[number + 1 :]
    fetch_window(pieces, swap_ref, q_ref.shape[0], window, sems)
    spans = head_spans(heads)
    grads[...] = jnp.zeros(grads.shape, F32)

    def query_block(i, carry):
        r = pl.multiple_of(i * QB, QB)
        dq_s[...] = jnp.zeros(dq_s.shape, F32)
        st = se_ref[0:1, pl.ds(r, QB)]
        en = se_ref[1:2, pl.ds(r, QB)]

        def chunk(c, inner):
            k0 = pl.multiple_of(lo_ref[i] + c * KB, 16)
            at = k0 + lax.broadcasted_iota(jnp.int32, (KB, QB), 0)
            mask = (at >= st) & (at < en)
            for h in range(heads):
                t, w, off = spans[h]
                ones = head_ones(w, off)
                q = q_ref[pl.ds(r, QB), t : t + w] * ones
                do = do_ref[pl.ds(r, QB), t : t + w] * ones
                k = window[pl.ds(k0, KB), t : t + w]
                v = window[pl.ds(k0, KB), W + t : W + t + w]
                s = dot_on(k, q, 1, 1)
                p = jnp.exp2(jnp.where(mask, s - lse_ref[h : h + 1, pl.ds(r, QB)], NEGATIVE))
                dp = dot_on(v, do, 1, 1)
                ds = (p * (dp - delta_ref[h : h + 1, pl.ds(r, QB)])).astype(BF)
                grads[pl.ds(k0, KB), W + t : W + t + w] += dot_on(p.astype(BF), do, 1, 0)
                grads[pl.ds(k0, KB), t : t + w] += dot_on(ds, q, 1, 0)
                dq_s[h, :, :w] += dot_on(ds, k, 0, 0)
            return inner

        lax.fori_loop(0, count_ref[i], chunk, 0)
        for h in range(heads):
            t, w, off = spans[h]
            dq = (dq_s[h, :, :w] * SCALE).astype(BF)
            dq_ref[pl.ds(r, QB), t : t + w] = jnp.where(
                in_head(QB, w, off), dq, dq_ref[pl.ds(r, QB), t : t + w]
            )
        return carry

    lax.fori_loop(0, q_ref.shape[0] // QB, query_block, 0)
    for ref, row, at, rows in window_parts(outs, swap_ref, q_ref.shape[0]):

        def store(j, carry, ref=ref, row=row, at=at):
            to = pl.multiple_of(row + j * 128, 128)
            here = pl.multiple_of(at + j * 128, 128)
            ref[pl.ds(to, 128), :W] = (grads[pl.ds(here, 128), :W] * math.log(2.0)).astype(BF)
            ref[pl.ds(to, 128), W:] = grads[pl.ds(here, 128), W:].astype(BF)
            return carry

        lax.fori_loop(0, rows // 128, store, 0)


def attend_backward(q, do, pieces, ranges, lse, delta, swap, heads, QB=256, KB=768):
    st, en = ranges
    FR, W = q.shape
    rows = 3 * FR + 2 * EDGE
    lo, count = key_chunks(st, en, QB, KB, rows)
    grads = [(piece, 2 * W) for piece in (FR, FR, FR, EDGE, EDGE)]
    return pl.pallas_call(
        functools.partial(backward_kernel, heads, W, QB, KB),
        out_shape=(jax.ShapeDtypeStruct((FR, W), BF),)
        + tuple(jax.ShapeDtypeStruct(shape, BF) for shape in grads),
        in_specs=[SMEM] * 3 + [VMEM] * 5 + [ANY] * len(pieces),
        out_specs=(VMEM,) * (1 + len(grads)),
        scratch_shapes=[
            pltpu.VMEM((rows, 2 * W), BF),
            pltpu.VMEM((rows, 2 * W), F32),
            pltpu.VMEM((heads, QB, 256), F32),
            pltpu.SemaphoreType.DMA((8,)),
        ],
        compiler_params=pltpu.CompilerParams(vmem_limit_bytes=60 << 20),
        cost_estimate=pl.CostEstimate(flops=0, bytes_accessed=0, transcendentals=0),
        name="attend_backward",
    )(lo, count, swap, jnp.stack((st, en)), lse, delta, q, do, *pieces)


def key_chunks(st, en, QB, KB, rows):
    lo = st[::QB] // 16 * 16
    count = (en[QB - 1 :: QB] - lo + KB - 1) // KB
    return jnp.minimum(lo, rows - count * KB), count


STEP = 256
FREE = pl.CostEstimate(flops=0, bytes_accessed=0, transcendentals=0)


def once(shape):
    return pl.BlockSpec(shape, lambda i: (0,) * len(shape), pipeline_mode=pl.Buffered(1))


def width_of(n, limit):
    return max(w for w in range(128, min(n, limit) + 1, 128) if n % w == 0)


def dense(xs, weights, n, product, finish, outs, extras=(), name="dense", width=512):
    weight, weight_spec = weights

    def kernel(*refs):
        x_refs, refs = refs[: len(xs)], refs[len(xs) :]
        w_ref, refs = refs[0], refs[1:]
        extra_refs, out_refs = refs[: len(extras)], refs[len(extras) :]
        w = w_ref[...].reshape(w_ref.shape[-2:])
        base = 0
        for x_ref in x_refs:
            for row in range(0, x_ref.shape[0], STEP):
                rows = min(STEP, x_ref.shape[0] - row)
                finish(product(x_ref[row : row + rows, :], w), base + row, extra_refs, out_refs)
            base += x_ref.shape[0]

    return pl.pallas_call(
        kernel,
        grid=(n // width,),
        in_specs=[once(x.shape) for x in xs] + [weight_spec] + [spec for _, spec in extras],
        out_specs=tuple(spec for _, _, spec in outs),
        out_shape=tuple(jax.ShapeDtypeStruct(shape, kind) for shape, kind, _ in outs),
        compiler_params=pltpu.CompilerParams(vmem_limit_bytes=50 << 20),
        cost_estimate=FREE,
        name=name,
    )(*xs, weight, *[x for x, _ in extras])


def count_rows(xs):
    return sum(x.shape[0] for x in xs)


def project_rows(xs, weight, first, n, bias, scale, name):
    weight, layer = weight
    rows, depth = count_rows(xs), weight.shape[1]
    width = math.gcd(width_of(n, 640), first) if first else width_of(n, 640)

    def finish(result, row, extra, out):
        out[0][row : row + result.shape[0], :] = ((result + extra[0][...]) * scale).astype(BF)

    return dense(
        xs,
        (weight, pl.BlockSpec((1, depth, width), lambda i: (layer, 0, i + first // width))),
        n,
        lambda x, w: dot_on(x, w, 1, 0),
        finish,
        [((rows, n), BF, pl.BlockSpec((rows, width), lambda i: (0, i)))],
        [(bias[None, :], pl.BlockSpec((1, width), lambda i: (0, i)))],
        name,
        width,
    )[0]


def widen_rows(xs, weight, bias):
    fc_all, layer = weight
    rows, depth, n = count_rows(xs), fc_all.shape[1], fc_all.shape[2]
    width = width_of(n, 512)

    def finish(result, row, extra, out):
        active, slope = gelu_both(result + extra[0][...])
        out[0][row : row + result.shape[0], :] = active
        out[1][row : row + result.shape[0], :] = slope

    spec = pl.BlockSpec((rows, width), lambda i: (0, i))
    return dense(
        xs,
        (fc_all, pl.BlockSpec((1, depth, width), lambda i: (layer, 0, i))),
        n,
        lambda x, w: dot_on(x, w, 1, 0),
        finish,
        [((rows, n), BF, spec)] * 2,
        [(bias[None, :], pl.BlockSpec((1, width), lambda i: (0, i)))],
        "widen",
        width,
    )


def slope_rows(xs, weight, slope):
    fc_all, layer = weight
    rows, depth, n = count_rows(xs), fc_all.shape[1], fc_all.shape[2]
    width = width_of(n, 512)

    def finish(result, row, extra, out):
        grad = (result * extra[0][row : row + result.shape[0], :].astype(F32)).astype(BF)
        out[0][row : row + result.shape[0], :] = grad
        total = jnp.sum(grad.astype(F32), axis=0, keepdims=True)
        out[1][...] = total if row == 0 else out[1][...] + total

    spec = pl.BlockSpec((rows, width), lambda i: (0, i))
    return dense(
        xs,
        (fc_all, pl.BlockSpec((1, depth, width), lambda i: (layer, 0, i))),
        n,
        lambda x, w: dot_on(x, w, 1, 0),
        finish,
        [((rows, n), BF, spec), ((1, n), F32, pl.BlockSpec((1, width), lambda i: (0, i)))],
        [(slope, spec)],
        "grad_hidden",
        width,
    )


def back_rows(xs, weight, columns, name):
    weight, layer = weight
    rows = xs[0].shape[0]
    n = weight.shape[-2]
    width = width_of(n, 256)
    half = rows // 2 if lax.axis_size("tensor") == 2 else 0
    depth = weight.shape[-1]

    def kernel(*refs):
        x_refs, w_ref, out_refs = refs[: len(xs)], refs[len(xs)], refs[len(xs) + 1 :]
        w = w_ref[...].reshape(w_ref.shape[-2:])
        for row in range(0, rows, STEP):
            result = sum(
                dot_on(x_ref[row : row + STEP, :], w[:, c : c + x_ref.shape[1]], 1, 1)
                for x_ref, c in zip(x_refs, columns)
            )
            if row < half:
                out_refs[0][row : row + STEP, :] = result
            else:
                out_refs[-1][row - half : row - half + STEP, :] = result.astype(BF)

    w_spec = pl.BlockSpec((1, width, depth), lambda i: (layer, i, 0))
    kinds = [(half, F32)] if half else []
    kinds.append((rows - half, BF))
    return pl.pallas_call(
        kernel,
        grid=(n // width,),
        in_specs=[once(x.shape) for x in xs] + [w_spec],
        out_specs=tuple(pl.BlockSpec((r, width), lambda i: (0, i)) for r, _ in kinds),
        out_shape=tuple(jax.ShapeDtypeStruct((r, n), kind) for r, kind in kinds),
        compiler_params=pltpu.CompilerParams(vmem_limit_bytes=50 << 20),
        cost_estimate=FREE,
        name=name,
    )(*xs, weight)


def weight_terms(parts, n, kind, start=None, place=None, room=52):
    depth = parts[0][1][0][0].shape[1]
    height = width_of(depth, 256)
    xs, ys = [], []
    plan = []
    for column, pairs in parts:
        for x, y, row in pairs:
            if not any(x is known for known in xs):
                xs.append(x)
            if not any(y is known for known in ys):
                ys.append(y)
        plan.append(
            (
                column,
                [
                    (
                        next(k for k, known in enumerate(xs) if known is x),
                        next(k for k, known in enumerate(ys) if known is y),
                        row,
                    )
                    for x, y, row in pairs
                ],
            )
        )
    more = []
    if start is not None:
        more.append(start)
    if place is not None and place[1] is not None:
        more.append(place[1])

    def kernel(*refs):
        x_refs, refs = refs[: len(xs)], refs[len(xs) :]
        y_refs, refs = refs[: len(ys)], refs[len(ys) :]
        out_ref = refs[-1]

        def store(a, b, value):
            if place is None:
                out_ref[:, a:b] = value.astype(kind)
            else:
                out_ref[0, :, a:b] = value.astype(kind)

        done = []
        for column, pairs in plan:
            span = y_refs[pairs[0][1]].shape[1]
            width = width_of(span, 640)
            for c in range(0, span, width):
                total = None if start is None else refs[0][:, column + c : column + c + width]
                for x, y, row in pairs:
                    count = x_refs[x].shape[0]
                    part = dot_on(x_refs[x][...], y_refs[y][row : row + count, c : c + width], 0, 0)
                    total = part if total is None else total + part
                store(column + c, column + c + width, total)
            done.append((column, column + span))
        edge = 0
        for a, b in sorted(done) + [(n, n)]:
            if a > edge:
                rest = jnp.zeros((height, a - edge), F32) if start is None else refs[0][:, edge:a]
                store(edge, a, rest)
            edge = b

    x_spec = [pl.BlockSpec((x.shape[0], height), lambda i: (0, i)) for x in xs]
    more_spec = []
    if start is not None:
        more_spec.append(pl.BlockSpec((height, n), lambda i: (i, 0)))
    aliases = {}
    if place is None:
        shape, spec = (depth, n), pl.BlockSpec((height, n), lambda i: (i, 0))
    else:
        slot = place[0]
        shape, spec = (2, depth, n), pl.BlockSpec((1, height, n), lambda i: (slot, i, 0))
        if place[1] is not None:
            more_spec.append(ANY)
            aliases = {len(xs) + len(ys) + len(more) - 1: 0}
    return pl.pallas_call(
        kernel,
        grid=(depth // height,),
        in_specs=x_spec + [once(y.shape) for y in ys] + more_spec,
        out_specs=spec,
        out_shape=jax.ShapeDtypeStruct(shape, kind),
        input_output_aliases=aliases,
        compiler_params=pltpu.CompilerParams(vmem_limit_bytes=room << 20),
        cost_estimate=FREE,
        name="weight_terms",
    )(*xs, *ys, *more)


def across(x):
    length = lax.axis_size("dp")
    pairs = [(i, i - 1 + 2 * (i % 2)) for i in range(length)]
    return lax.ppermute(x, "dp", [(i, j) for i, j in pairs if 0 <= j < length])


def inside(x):
    return lax.ppermute(x, "dp", [(i, i ^ 1) for i in range(lax.axis_size("dp"))])


def over_dp(x, by, start=0, step=1):
    length = lax.axis_size("dp")
    pairs = [(i, i + by) for i in range(start, length, step) if 0 <= i + by < length]
    return lax.ppermute(x, "dp", pairs)


def near_rows(kv, swap):
    half = kv.shape[0] // 2

    def head(x):
        return lax.dynamic_slice_in_dim(x, swap * half, EDGE)

    def tail(x):
        return lax.dynamic_slice_in_dim(x, (1 - swap) * half, EDGE)

    left, right = over_dp(kv, 1), over_dp(kv, -1)
    far_left, far_right = over_dp(tail(kv), 2, 0, 2), over_dp(head(kv), -2, 1, 2)
    return (
        far_left,
        over_dp(tail(left), 1, 0, 2),
        left,
        kv,
        right,
        far_right,
        over_dp(head(right), -1, 1, 2),
    )


BLOCK = 256


def add_far(near, far, second):
    rows, width = far.shape
    steps = rows // BLOCK

    def kernel(second_ref, near_ref, far_ref, out_ref):
        out_ref[...] = (near_ref[...].astype(F32) + far_ref[...].astype(F32)).astype(BF)

    here = pl.BlockSpec((BLOCK, width), lambda i, s: (s[0] * steps + i, 0))
    return pl.pallas_call(
        kernel,
        grid_spec=pltpu.PrefetchScalarGridSpec(
            num_scalar_prefetch=1,
            grid=(steps,),
            in_specs=[here, pl.BlockSpec((BLOCK, width), lambda i, s: (i, 0))],
            out_specs=here,
        ),
        out_shape=jax.ShapeDtypeStruct(near.shape, BF),
        input_output_aliases={1: 0},
        cost_estimate=FREE,
        name="add_far",
    )(second[None], near, far)


def return_rows(grads, place):
    swap, core = place[0], place[1]
    near_inside, near_across, own, far_across, far_inside = grads
    head, tail = swap, 1 - swap
    near_across = add_far(near_across, inside(far_inside), jnp.where(core == 0, tail, head))
    from_across = across(near_across)
    near_inside = add_far(near_inside, across(far_across), jnp.where(core == 0, head, tail))
    return (own, from_across, inside(near_inside)), near_across


def add_returned(parts):
    rows, width = parts[0].shape

    def kernel(*refs):
        refs[-1][...] = sum(ref[...].astype(F32) for ref in refs[:-1]).astype(BF)

    block = pl.BlockSpec((BLOCK, width), lambda i: (i, 0))
    return pl.pallas_call(
        kernel,
        grid=(rows // BLOCK,),
        in_specs=[block] * len(parts),
        out_specs=block,
        out_shape=jax.ShapeDtypeStruct((rows, width), BF),
        cost_estimate=FREE,
        name="add_returned",
    )(*parts)


def sum_everywhere(x, axis):
    length = lax.axis_size(axis)
    bit = 1
    while bit < length:
        x = x + lax.ppermute(x, axis, [(i, i ^ bit) for i in range(length)])
        bit *= 2
    return x


class Order:
    def __init__(self):
        self.last = None

    def after(self, x, *more):
        if self.last is not None:
            more += (self.last,)
        return lax.optimization_barrier((x, *more))[0] if more else x

    def done(self, x):
        self.last = x
        return x


def partner(x):
    return lax.ppermute(x, "tensor", [(0, 1), (1, 0)])


def collect(x):
    if lax.axis_size("tensor") != 2:
        return [lax.all_gather(x, "tensor", axis=0, tiled=True)]
    return [x, partner(x)]


def share(parts):
    if len(parts) == 1:
        return lax.psum_scatter(parts[0], "tensor", scatter_dimension=0, tiled=True), jnp.zeros((), BF)
    return parts[0], partner(parts[1])


def norm_parts(x):
    centred = x - jnp.mean(x, axis=-1, keepdims=True)
    scale = lax.rsqrt(jnp.mean(centred * centred, axis=-1, keepdims=True) + EPSILON)
    return centred * scale, scale


def norm_back_rows(near, far, x, gain, base):
    rows, width = near.shape
    step = math.gcd(rows, 128)
    far = jnp.broadcast_to(far, near.shape)

    def kernel(near_ref, far_ref, x_ref, gain_ref, base_ref, out_ref, low_ref, sums_ref):
        grad = near_ref[...].astype(F32) + far_ref[...].astype(F32)
        z, scale = norm_parts(x_ref[...].astype(F32))
        e = grad * gain_ref[...]
        mean_e = jnp.mean(e, axis=-1, keepdims=True)
        mean_ez = jnp.mean(e * z, axis=-1, keepdims=True)
        before = base_ref[...].astype(F32)
        result = before + scale * (e - mean_e - z * mean_ez)
        out_ref[...] = result
        low_ref[...] = result.astype(BF)

        @pl.when(pl.program_id(0) == 0)
        def _():
            sums_ref[...] = jnp.zeros(sums_ref.shape, F32)

        for row, part in enumerate((grad * z, grad, result, before)):
            sums_ref[row : row + 1, :] += jnp.sum(part, axis=0, keepdims=True)

    block = pl.BlockSpec((step, width), lambda i: (i, 0))
    return pl.pallas_call(
        kernel,
        grid=(rows // step,),
        in_specs=[block, block, block, pl.BlockSpec((1, width), lambda i: (0, 0)), block],
        out_specs=(block, block, pl.BlockSpec((8, width), lambda i: (0, 0))),
        out_shape=(
            jax.ShapeDtypeStruct((rows, width), F32),
            jax.ShapeDtypeStruct((rows, width), BF),
            jax.ShapeDtypeStruct((8, width), F32),
        ),
        compiler_params=pltpu.CompilerParams(vmem_limit_bytes=26 << 20),
        cost_estimate=FREE,
        name="norm_back",
    )(near, far, x, gain[None, :], base)


def gelu_both(u):
    below = 0.5 * (1.0 + lax.erf(u * math.sqrt(0.5)))
    density = jnp.exp(-0.5 * u * u) * (1.0 / math.sqrt(2.0 * math.pi))
    return (u * below).astype(BF), (below + u * density).astype(BF)


def per_device(
    frames, cotangent, segment_ids, w_qkv, w_out, w_fc1, w_fc2, bias_qv, bias_fc1, norm_vectors
):
    dp_place = lax.axis_index("dp")
    paired = lax.axis_size("tensor") == 2
    swap = lax.axis_index("tensor").astype(jnp.int32) if paired else jnp.int32(0)
    own = frames.shape[1]
    FR = own * lax.axis_size("tensor")
    half = FR // 2
    rows = 2 * EDGE + 3 * FR
    local = w_qkv.shape[2]
    heads = local // HD
    W = -(-local // 128) * 128
    fill = W - local
    vectors = norm_vectors.astype(F32)

    def widened(x):
        return jnp.pad(x, [(0, 0)] * (x.ndim - 1) + [(0, fill)]) if fill else x

    attention = jnp.concatenate(
        (widened(w_qkv).reshape(w_qkv.shape[0], 3 * W), widened(w_out)), axis=1
    )
    att = lax.all_gather(attention[None], "dp", axis=1, tiled=True), 0
    bias_q = widened(bias_qv[0].astype(F32))
    bias_kv = jnp.concatenate((jnp.zeros((W,), F32), widened(bias_qv[1].astype(F32))))
    chosen = (jnp.arange(W)[:, None] // HD == jnp.arange(heads)[None, :]).astype(F32)
    order = Order()

    class Batch:
        pass

    batches = []
    for b in range(MB):
        m = Batch()
        batches.append(m)
        m.z1, m.r1 = norm_parts(frames[b].astype(F32))
        m.h1_own = (m.z1 * vectors[0] + vectors[1]).astype(BF)
        ids = segment_ids[b]
        reach = FR + EDGE
        padded = jnp.concatenate(
            (jnp.full((reach,), -1, jnp.int32), ids, jnp.full((reach,), 1 << 30, jnp.int32))
        )
        near = lax.dynamic_slice_in_dim(padded, dp_place * FR, rows)
        mine = jnp.concatenate(
            (
                lax.dynamic_slice_in_dim(ids, dp_place * FR + swap * half, half),
                lax.dynamic_slice_in_dim(ids, dp_place * FR + (1 - swap) * half, half),
            )
        )
        m.ranges = (
            jnp.sum((near[None, :] < mine[:, None]).astype(jnp.int32), axis=1),
            jnp.sum((near[None, :] <= mine[:, None]).astype(jnp.int32), axis=1),
        )
    m0, m1 = batches
    place = jnp.stack((swap, dp_place.astype(jnp.int32) % 2))
    for m in batches:
        m.h1 = collect(m.h1_own)

    def gated(xs, *wait):
        *rest, x = xs
        return [*rest, order.after(x, *wait)]

    def keys_values(m, *wait):
        m.kv = order.done(project_rows(gated(m.h1, *wait), att, W, 2 * W, bias_kv, 1.0, "keys_values"))

    def queries(m):
        m.q = order.done(project_rows(gated(m.h1), att, 0, W, bias_q, LOG2E * SCALE, "queries"))

    def attend(m, *wait):
        m.mixed, m.lse = attend_forward(order.after(m.q, *wait), m.pieces, m.ranges, place, heads)
        order.done(m.mixed)
        parts = back_rows([m.mixed], att, [3 * W], "attended")
        m.attended, m.attended_far = share(parts)
        order.done(parts[0])

    def second_norm(m):
        near, far = m.attended, order.after(m.attended_far)
        m.middle = frames[m.b].astype(F32) + near.astype(F32) + far.astype(F32) + vectors[4]
        m.z2, m.r2 = norm_parts(m.middle)
        h2 = order.done((m.z2 * vectors[2] + vectors[3]).astype(BF))
        m.h2 = collect(h2)

    def widen(m):
        m.active, m.slope = widen_rows(gated(m.h2), fc1, bias_fc1.astype(F32))
        order.done(m.slope)

    def grad_hidden(m):
        m.grad_u, m.grad_u_sum = slope_rows(gated(m.grad_f), fc2, m.slope)
        order.done(m.grad_u)

    def grad_normed(m):
        parts = back_rows(gated([m.grad_u]), fc1, [0], "grad_normed")
        m.grad_h2, m.grad_h2_far = share(parts)
        order.done(parts[0])

    def narrow(m, *wait):
        m.fed_parts = back_rows(gated([m.active], *wait), fc2, [0], "narrow")
        order.done(m.fed_parts[0])

    def send_narrow(m):
        *rest, last = m.fed_parts
        m.fed, m.fed_far = share([*rest, order.after(last)])

    def grad_second_norm(m):
        m.grad_middle, a, m.sums_two = norm_back_rows(
            m.grad_h2, order.after(m.grad_h2_far), m.middle, vectors[2], cotangent[m.b]
        )
        m.grad_a = collect(order.done(a))

    no_bias = jnp.zeros((W,), F32)

    def attend_back(m, *wait):
        m.grad_mixed = project_rows(
            gated(m.grad_a), att, 3 * W, W, no_bias, 1.0, "grad_mixed"
        )
        delta = lax.dot_general(
            chosen,
            m.grad_mixed.astype(F32) * m.mixed.astype(F32),
            (((0,), (1,)), ((), ())),
            precision=lax.Precision.HIGHEST,
        )
        m.grad_q, *grads = attend_backward(
            lax.optimization_barrier((m.q, *wait))[0] if wait else m.q, m.grad_mixed, m.pieces, m.ranges, m.lse, delta, place, heads
        )
        order.done(m.grad_q)
        m.grads = grads

    def send_back(m):
        near_inside, near_across, *rest = m.grads
        m.returned, m.ready = return_rows([near_inside, order.after(near_across), *rest], place)

    def add_up(m, *wait):
        m.grad_kv = order.done(add_returned([order.after(x, *wait) for x in m.returned]))

    def grad_projected(m):
        grad_kv = order.after(m.grad_kv)
        parts = back_rows([m.grad_q, grad_kv], att, [0, W], "grad_projected")
        m.grad_h1, m.grad_h1_far = share(parts)
        order.done(parts[0])

    def rows_of(xs, y):
        pairs, row = [], 0
        for x in xs:
            pairs.append((x, y, row))
            row += x.shape[0]
        return pairs

    def finish(m):
        m.inputs_grad, low, sums_one = norm_back_rows(
            m.grad_h1, order.after(m.grad_h1_far), frames[m.b], vectors[0], m.grad_middle
        )
        order.done(low)
        m.norm_sums = jnp.concatenate((sums_one[:2], m.sums_two[:4]))

    def owned(terms, axis):
        return lax.psum_scatter(terms.astype(BF), "dp", scatter_dimension=axis, tiled=True).astype(F32)

    m0.b, m1.b = 0, 1
    keys_values(m0, m1.h1[-1])
    keys_values(m1)
    queries(m0)
    queries(m1)
    m0.pieces = near_rows(m0.kv, swap)
    first_arrived = [m0.pieces[k] for k in (0, 2, 4, 5)]
    w_fc = lax.optimization_barrier((jnp.stack((w_fc1, w_fc2)), *first_arrived))[0]
    fc_all = lax.all_gather(w_fc, "dp", axis=1, tiled=True)
    fc1, fc2 = (fc_all, 0), (fc_all, 1)
    m1.pieces = near_rows(lax.optimization_barrier((m1.kv, m1.q, *first_arrived))[0], swap)
    for m in batches:
        m.grad_f = collect(lax.optimization_barrier((cotangent[m.b], m1.h1[-1]))[0])

    def term(x, y, *wait, **how):
        pairs = rows_of(gated(x, *wait), y)
        return order.done(weight_terms([(0, pairs)], w_fc1.shape[1], **how))

    attend(m0, m0.grad_f[-1], m1.grad_f[-1])
    second_norm(m0)
    attend(m1)
    widen(m0)
    grad_hidden(m0)
    grad_normed(m0)
    second_norm(m1)
    narrow(m0)
    fc2_term = term(m0.grad_f, m0.active, kind=F32)
    grad_second_norm(m0)
    fc1_term = term(m0.h2, m0.grad_u, kind=F32)
    widen(m1)
    grad_hidden(m1)
    grad_normed(m1)
    fc_terms = term(
        m1.grad_f, m1.active, m0.grad_a[-1], kind=BF, start=fc2_term, place=(1, None)
    )
    grad_second_norm(m1)
    fc_terms = term(m1.h2, m1.grad_u, kind=BF, start=fc1_term, place=(0, fc_terms))
    own_fc1, own_fc2 = owned(fc_terms, 1)
    attend_back(m0)
    send_back(m0)
    send_narrow(m0)
    attend_back(m1, m0.ready)
    narrow(m1, m0.fed_far)
    send_narrow(m1)
    terms = weight_terms(
        [
            (0, rows_of(gated(m0.h1), m0.grad_q) + rows_of(m1.h1, m1.grad_q)),
            (3 * W, rows_of(m0.grad_a, m0.mixed) + rows_of(m1.grad_a, m1.mixed)),
        ],
        4 * W,
        F32,
    )
    order.done(terms)
    send_back(m1)
    add_up(m0, m1.ready)
    grad_projected(m0)
    add_up(m1, m1.fed_far)
    kv_pairs = rows_of(m0.h1, m0.grad_kv) + rows_of(gated(m1.h1), m1.grad_kv)
    terms = order.done(weight_terms([(W, kv_pairs)], 4 * W, BF, start=terms, room=26))
    grad_projected(m1)
    own_attention = owned(lax.optimization_barrier((terms, own_fc1))[0], 0)
    finish(m0)
    outputs = [
        (m.middle + m.fed.astype(F32) + order.after(m.fed_far).astype(F32) + vectors[5]).astype(BF)
        for m in batches
    ]
    finish(m1)
    own_qkv = own_attention[:, : 3 * W].reshape(own_attention.shape[0], 3, W)[:, :, :local]
    own_out = own_attention[:, 3 * W :][:, :local]

    bias_parts = (
        sum(jnp.sum(m.grad_q, axis=0, dtype=F32) for m in batches)[:local],
        sum(jnp.sum(m.grad_kv[:, W:], axis=0, dtype=F32) for m in batches)[:local],
        sum(m.grad_u_sum[0] for m in batches),
    )
    norm_sums = m0.norm_sums + m1.norm_sums
    small = sum_everywhere(jnp.concatenate(bias_parts + (norm_sums.reshape(-1),)), "dp")
    bias_qv_total = small[: 2 * local].reshape(2, local)
    bias_fc1_total = small[2 * local : 2 * local + w_fc1.shape[1]]
    norm_total = sum_everywhere(small[2 * local + w_fc1.shape[1] :], "tensor").reshape(norm_sums.shape)
    return (
        jnp.stack(outputs),
        jnp.stack([m.inputs_grad for m in batches]),
        own_qkv,
        own_out,
        own_fc1,
        own_fc2,
        bias_qv_total,
        bias_fc1_total,
        norm_total,
    )


def solution(mesh):
    in_specs = (
        P(None, ("dp", "tensor"), None),
        P(None, ("dp", "tensor"), None),
        P(),
        P("dp", None, "tensor"),
        P("dp", "tensor"),
        P("dp", "tensor"),
        P("dp", "tensor"),
        P(None, "tensor"),
        P("tensor"),
        P(),
    )
    out_specs = (
        P(None, ("dp", "tensor"), None),
        P(None, ("dp", "tensor"), None),
        P("dp", None, "tensor"),
        P("dp", "tensor"),
        P("dp", "tensor"),
        P("dp", "tensor"),
        P(None, "tensor"),
        P("tensor"),
        P(),
    )
    return jax.shard_map(
        per_device, mesh=mesh, in_specs=in_specs, out_specs=out_specs, check_vma=False
    )
```

```python
import functools
import math

import jax
import jax.numpy as jnp
from jax import lax
from jax.experimental import pallas as pl
from jax.experimental.pallas import tpu as pltpu
from jax.sharding import PartitionSpec as P

HD = 80
MB = 2
EDGE = 512
EPSILON = 1e-05
NEGATIVE = -1e30
LOG2E = math.log2(math.e)
SCALE = 1.0 / math.sqrt(HD)
BF = jnp.bfloat16
F32 = jnp.float32


def head_spans(heads):
    spans = []
    for head in range(heads):
        first, last = head * HD, (head + 1) * HD
        start = first // 128 * 128
        spans.append((start, -(-last // 128) * 128 - start, first - start))
    return spans


def dot_on(a, b, a_dim, b_dim):
    return lax.dot_general(a, b, (((a_dim,), (b_dim,)), ((), ())), preferred_element_type=F32)


def in_head(rows, width, offset):
    lane = lax.broadcasted_iota(jnp.int32, (rows, width), 1)
    return (lane >= offset) & (lane < offset + HD)


def head_ones(width, offset):
    return jnp.where(in_head(1, width, offset), 1.0, 0.0).astype(BF)


def window_parts(refs, place, FR):
    swap, core = place[0], place[1]
    half = FR // 2
    left, right, last = EDGE, EDGE + 2 * FR, EDGE + 3 * FR
    inside, across = right + core * (left - right), left + core * (right - left)
    parts = []
    for ref, base in zip(refs[:3], (inside, across, EDGE + FR)):
        parts.append((ref, 0, base + swap * half, half))
        parts.append((ref, half, base + (1 - swap) * half, half))
    parts.append((refs[3], 0, core * last, EDGE))
    parts.append((refs[4], 0, (1 - core) * last, EDGE))
    return parts


def piece_parts(refs, swap, FR):
    half = FR // 2
    both = (swap * half, (1 - swap) * half)
    bases = [[base + add for add in both] for base in (EDGE, EDGE + FR, EDGE + 2 * FR)]
    bases = [[0]] + bases + [[EDGE + 3 * FR]]
    return [
        (ref, number * half, base, half)
        for ref, group in zip(refs, bases)
        for number, base in enumerate(group)
    ]


def fetch_window(refs, place, FR, window, sems):
    swap, core = place[0], place[1]
    left_direct, left_relayed, *near, right_direct, right_relayed = refs
    copies = []
    for number, (ref, row, at, rows) in enumerate(piece_parts([left_direct, *near, right_direct], swap, FR)):
        to = window.at[pl.ds(pl.multiple_of(at, EDGE), rows)]
        copies.append(pltpu.make_async_copy(ref.at[pl.ds(row, rows)], to, sems.at[number]))
        if ref is left_direct or ref is right_direct:
            other = pltpu.make_async_copy(
                left_relayed if ref is left_direct else right_relayed, to, sems.at[number]
            )
            here = core == (0 if ref is left_direct else 1)
            pl.when(here)(copies[-1].start)
            pl.when(jnp.logical_not(here))(other.start)
        else:
            copies[-1].start()
    for copy in copies:
        copy.wait()


def forward_kernel(heads, W, QB, KB, lo_ref, count_ref, place_ref, se_ref, q_ref, *refs):
    *pieces, o_ref, lse_ref, window, sems, top_s, sum_s, acc_s = refs
    fetch_window(pieces, place_ref, q_ref.shape[0], window, sems)
    spans = head_spans(heads)

    def query_block(i, carry):
        r = pl.multiple_of(i * QB, QB)
        top_s[...] = jnp.full(top_s.shape, NEGATIVE, F32)
        sum_s[...] = jnp.zeros(sum_s.shape, F32)
        acc_s[...] = jnp.zeros(acc_s.shape, F32)
        st = se_ref[0:1, pl.ds(r, QB)]
        en = se_ref[1:2, pl.ds(r, QB)]

        def chunk(c, inner):
            k0 = pl.multiple_of(lo_ref[i] + c * KB, 16)
            at = k0 + lax.broadcasted_iota(jnp.int32, (KB, QB), 0)
            mask = (at >= st) & (at < en)
            for h in range(heads):
                t, w, off = spans[h]
                q = q_ref[pl.ds(r, QB), t : t + w] * head_ones(w, off)
                v = window[pl.ds(k0, KB), W + t : W + t + w]
                s = dot_on(window[pl.ds(k0, KB), t : t + w], q, 1, 1)
                s = jnp.where(mask, s, NEGATIVE)
                before = top_s[h : h + 1, :]
                top = jnp.maximum(before, jnp.max(s, axis=0, keepdims=True))
                p = jnp.exp2(s - top)
                shrink = jnp.exp2(before - top)
                sum_s[h : h + 1, :] = sum_s[h : h + 1, :] * shrink + jnp.sum(p, axis=0, keepdims=True)
                acc_s[h, :w, :] = acc_s[h, :w, :] * shrink + dot_on(v, p.astype(BF), 0, 0)
                top_s[h : h + 1, :] = top
            return inner

        lax.fori_loop(0, count_ref[i], chunk, 0)
        for h in range(heads):
            t, w, off = spans[h]
            o = (acc_s[h, :w, :] / sum_s[h : h + 1, :]).T.astype(BF)
            o_ref[pl.ds(r, QB), t : t + w] = jnp.where(
                in_head(QB, w, off), o, o_ref[pl.ds(r, QB), t : t + w]
            )
        lse_ref[:, pl.ds(r, QB)] = top_s[...] + jnp.log2(sum_s[...])
        return carry

    lax.fori_loop(0, q_ref.shape[0] // QB, query_block, 0)


SMEM = pl.BlockSpec(memory_space=pltpu.SMEM)
VMEM = pl.BlockSpec(memory_space=pltpu.VMEM)
ANY = pl.BlockSpec(memory_space=pl.ANY)


def attend_forward(q, pieces, ranges, swap, heads, QB=256, KB=1536):
    st, en = ranges
    FR, W = q.shape
    rows = 3 * FR + 2 * EDGE
    lo, count = key_chunks(st, en, QB, KB, rows)
    return pl.pallas_call(
        functools.partial(forward_kernel, heads, W, QB, KB),
        out_shape=(
            jax.ShapeDtypeStruct((FR, W), BF),
            jax.ShapeDtypeStruct((heads, FR), F32),
        ),
        in_specs=[SMEM] * 3 + [VMEM] * 2 + [ANY] * len(pieces),
        out_specs=(VMEM, VMEM),
        scratch_shapes=[
            pltpu.VMEM((rows, 2 * W), BF),
            pltpu.SemaphoreType.DMA((8,)),
            pltpu.VMEM((heads, QB), F32),
            pltpu.VMEM((heads, QB), F32),
            pltpu.VMEM((heads, 256, QB), F32),
        ],
        compiler_params=pltpu.CompilerParams(vmem_limit_bytes=56 << 20),
        cost_estimate=pl.CostEstimate(flops=0, bytes_accessed=0, transcendentals=0),
        name="attend_forward",
    )(lo, count, swap, jnp.stack((st, en)), q, *pieces)


def backward_kernel(
    heads, W, QB, KB, lo_ref, count_ref, swap_ref, se_ref, lse_ref, delta_ref, q_ref, do_ref, *refs
):
    *refs, window, grads, dq_s, sems = refs
    number = len(refs) - 6
    pieces, dq_ref, outs = refs[:number], refs[number], refs[number + 1 :]
    fetch_window(pieces, swap_ref, q_ref.shape[0], window, sems)
    spans = head_spans(heads)
    grads[...] = jnp.zeros(grads.shape, F32)

    def query_block(i, carry):
        r = pl.multiple_of(i * QB, QB)
        dq_s[...] = jnp.zeros(dq_s.shape, F32)
        st = se_ref[0:1, pl.ds(r, QB)]
        en = se_ref[1:2, pl.ds(r, QB)]

        def chunk(c, inner):
            k0 = pl.multiple_of(lo_ref[i] + c * KB, 16)
            at = k0 + lax.broadcasted_iota(jnp.int32, (KB, QB), 0)
            mask = (at >= st) & (at < en)
            for h in range(heads):
                t, w, off = spans[h]
                ones = head_ones(w, off)
                q = q_ref[pl.ds(r, QB), t : t + w] * ones
                do = do_ref[pl.ds(r, QB), t : t + w] * ones
                k = window[pl.ds(k0, KB), t : t + w]
                v = window[pl.ds(k0, KB), W + t : W + t + w]
                s = dot_on(k, q, 1, 1)
                p = jnp.exp2(jnp.where(mask, s - lse_ref[h : h + 1, pl.ds(r, QB)], NEGATIVE))
                dp = dot_on(v, do, 1, 1)
                ds = (p * (dp - delta_ref[h : h + 1, pl.ds(r, QB)])).astype(BF)
                grads[pl.ds(k0, KB), W + t : W + t + w] += dot_on(p.astype(BF), do, 1, 0)
                grads[pl.ds(k0, KB), t : t + w] += dot_on(ds, q, 1, 0)
                dq_s[h, :, :w] += dot_on(ds, k, 0, 0)
            return inner

        lax.fori_loop(0, count_ref[i], chunk, 0)
        for h in range(heads):
            t, w, off = spans[h]
            dq = (dq_s[h, :, :w] * SCALE).astype(BF)
            dq_ref[pl.ds(r, QB), t : t + w] = jnp.where(
                in_head(QB, w, off), dq, dq_ref[pl.ds(r, QB), t : t + w]
            )
        return carry

    lax.fori_loop(0, q_ref.shape[0] // QB, query_block, 0)
    for ref, row, at, rows in window_parts(outs, swap_ref, q_ref.shape[0]):

        def store(j, carry, ref=ref, row=row, at=at):
            to = pl.multiple_of(row + j * 128, 128)
            here = pl.multiple_of(at + j * 128, 128)
            ref[pl.ds(to, 128), :W] = (grads[pl.ds(here, 128), :W] * math.log(2.0)).astype(BF)
            ref[pl.ds(to, 128), W:] = grads[pl.ds(here, 128), W:].astype(BF)
            return carry

        lax.fori_loop(0, rows // 128, store, 0)


def attend_backward(q, do, pieces, ranges, lse, delta, swap, heads, QB=256, KB=768):
    st, en = ranges
    FR, W = q.shape
    rows = 3 * FR + 2 * EDGE
    lo, count = key_chunks(st, en, QB, KB, rows)
    grads = [(piece, 2 * W) for piece in (FR, FR, FR, EDGE, EDGE)]
    return pl.pallas_call(
        functools.partial(backward_kernel, heads, W, QB, KB),
        out_shape=(jax.ShapeDtypeStruct((FR, W), BF),)
        + tuple(jax.ShapeDtypeStruct(shape, BF) for shape in grads),
        in_specs=[SMEM] * 3 + [VMEM] * 5 + [ANY] * len(pieces),
        out_specs=(VMEM,) * (1 + len(grads)),
        scratch_shapes=[
            pltpu.VMEM((rows, 2 * W), BF),
            pltpu.VMEM((rows, 2 * W), F32),
            pltpu.VMEM((heads, QB, 256), F32),
            pltpu.SemaphoreType.DMA((8,)),
        ],
        compiler_params=pltpu.CompilerParams(vmem_limit_bytes=60 << 20),
        cost_estimate=pl.CostEstimate(flops=0, bytes_accessed=0, transcendentals=0),
        name="attend_backward",
    )(lo, count, swap, jnp.stack((st, en)), lse, delta, q, do, *pieces)


def key_chunks(st, en, QB, KB, rows):
    lo = st[::QB] // 16 * 16
    count = (en[QB - 1 :: QB] - lo + KB - 1) // KB
    return jnp.minimum(lo, rows - count * KB), count


STEP = 256
FREE = pl.CostEstimate(flops=0, bytes_accessed=0, transcendentals=0)


def once(shape):
    return pl.BlockSpec(shape, lambda i: (0,) * len(shape), pipeline_mode=pl.Buffered(1))


def width_of(n, limit):
    return max(w for w in range(128, min(n, limit) + 1, 128) if n % w == 0)


def dense(xs, weights, n, product, finish, outs, extras=(), name="dense", width=512):
    weight, weight_spec = weights

    def kernel(*refs):
        x_refs, refs = refs[: len(xs)], refs[len(xs) :]
        w_ref, refs = refs[0], refs[1:]
        extra_refs, out_refs = refs[: len(extras)], refs[len(extras) :]
        w = w_ref[...].reshape(w_ref.shape[-2:])
        base = 0
        for x_ref in x_refs:
            for row in range(0, x_ref.shape[0], STEP):
                rows = min(STEP, x_ref.shape[0] - row)
                finish(product(x_ref[row : row + rows, :], w), base + row, extra_refs, out_refs)
            base += x_ref.shape[0]

    return pl.pallas_call(
        kernel,
        grid=(n // width,),
        in_specs=[once(x.shape) for x in xs] + [weight_spec] + [spec for _, spec in extras],
        out_specs=tuple(spec for _, _, spec in outs),
        out_shape=tuple(jax.ShapeDtypeStruct(shape, kind) for shape, kind, _ in outs),
        compiler_params=pltpu.CompilerParams(vmem_limit_bytes=(26 if weight.shape[0] == 1 else 50) << 20),
        cost_estimate=FREE,
        name=name,
    )(*xs, weight, *[x for x, _ in extras])


def count_rows(xs):
    return sum(x.shape[0] for x in xs)


def project_rows(xs, weight, first, n, bias, scale, name):
    weight, layer = weight
    rows, depth = count_rows(xs), weight.shape[1]
    width = math.gcd(width_of(n, 640), first) if first else width_of(n, 640)

    def finish(result, row, extra, out):
        out[0][row : row + result.shape[0], :] = ((result + extra[0][...]) * scale).astype(BF)

    return dense(
        xs,
        (weight, pl.BlockSpec((1, depth, width), lambda i: (layer, 0, i + first // width))),
        n,
        lambda x, w: dot_on(x, w, 1, 0),
        finish,
        [((rows, n), BF, pl.BlockSpec((rows, width), lambda i: (0, i)))],
        [(bias[None, :], pl.BlockSpec((1, width), lambda i: (0, i)))],
        name,
        width,
    )[0]


def widen_rows(xs, weight, bias):
    fc_all, layer = weight
    rows, depth, n = count_rows(xs), fc_all.shape[1], fc_all.shape[2]
    width = width_of(n, 512)

    def finish(result, row, extra, out):
        active, slope = gelu_both(result + extra[0][...])
        out[0][row : row + result.shape[0], :] = active
        out[1][row : row + result.shape[0], :] = slope

    spec = pl.BlockSpec((rows, width), lambda i: (0, i))
    return dense(
        xs,
        (fc_all, pl.BlockSpec((1, depth, width), lambda i: (layer, 0, i))),
        n,
        lambda x, w: dot_on(x, w, 1, 0),
        finish,
        [((rows, n), BF, spec)] * 2,
        [(bias[None, :], pl.BlockSpec((1, width), lambda i: (0, i)))],
        "widen",
        width,
    )


def slope_rows(xs, weight, slope):
    fc_all, layer = weight
    rows, depth, n = count_rows(xs), fc_all.shape[1], fc_all.shape[2]
    width = width_of(n, 512)

    def finish(result, row, extra, out):
        grad = (result * extra[0][row : row + result.shape[0], :].astype(F32)).astype(BF)
        out[0][row : row + result.shape[0], :] = grad
        total = jnp.sum(grad.astype(F32), axis=0, keepdims=True)
        out[1][...] = total if row == 0 else out[1][...] + total

    spec = pl.BlockSpec((rows, width), lambda i: (0, i))
    return dense(
        xs,
        (fc_all, pl.BlockSpec((1, depth, width), lambda i: (layer, 0, i))),
        n,
        lambda x, w: dot_on(x, w, 1, 0),
        finish,
        [((rows, n), BF, spec), ((1, n), F32, pl.BlockSpec((1, width), lambda i: (0, i)))],
        [(slope, spec)],
        "grad_hidden",
        width,
    )


def back_rows(xs, weight, columns, name):
    weight, layer = weight
    rows = xs[0].shape[0]
    n = weight.shape[-2]
    width = width_of(n, 256)
    half = rows // 2 if lax.axis_size("tensor") == 2 else 0
    depth = weight.shape[-1]

    def kernel(*refs):
        x_refs, w_ref, out_refs = refs[: len(xs)], refs[len(xs)], refs[len(xs) + 1 :]
        w = w_ref[...].reshape(w_ref.shape[-2:])
        for row in range(0, rows, STEP):
            result = sum(
                dot_on(x_ref[row : row + STEP, :], w[:, c : c + x_ref.shape[1]], 1, 1)
                for x_ref, c in zip(x_refs, columns)
            )
            if row < half:
                out_refs[0][row : row + STEP, :] = result
            else:
                out_refs[-1][row - half : row - half + STEP, :] = result.astype(BF)

    w_spec = pl.BlockSpec((1, width, depth), lambda i: (layer, i, 0))
    kinds = [(half, F32)] if half else []
    kinds.append((rows - half, BF))
    return pl.pallas_call(
        kernel,
        grid=(n // width,),
        in_specs=[once(x.shape) for x in xs] + [w_spec],
        out_specs=tuple(pl.BlockSpec((r, width), lambda i: (0, i)) for r, _ in kinds),
        out_shape=tuple(jax.ShapeDtypeStruct((r, n), kind) for r, kind in kinds),
        compiler_params=pltpu.CompilerParams(vmem_limit_bytes=(26 if weight.shape[0] == 1 else 50) << 20),
        cost_estimate=FREE,
        name=name,
    )(*xs, weight)


def weight_terms(parts, n, kind, start=None, place=None, room=52):
    depth = parts[0][1][0][0].shape[1]
    height = width_of(depth, 256)
    xs, ys = [], []
    plan = []
    for column, pairs in parts:
        for x, y, row in pairs:
            if not any(x is known for known in xs):
                xs.append(x)
            if not any(y is known for known in ys):
                ys.append(y)
        plan.append(
            (
                column,
                [
                    (
                        next(k for k, known in enumerate(xs) if known is x),
                        next(k for k, known in enumerate(ys) if known is y),
                        row,
                    )
                    for x, y, row in pairs
                ],
            )
        )
    more = []
    if start is not None:
        more.append(start)
    if place is not None and place[1] is not None:
        more.append(place[1])

    def kernel(*refs):
        x_refs, refs = refs[: len(xs)], refs[len(xs) :]
        y_refs, refs = refs[: len(ys)], refs[len(ys) :]
        out_ref = refs[-1]

        def store(a, b, value):
            if place is None:
                out_ref[:, a:b] = value.astype(kind)
            else:
                out_ref[0, :, a:b] = value.astype(kind)

        done = []
        for column, pairs in plan:
            span = y_refs[pairs[0][1]].shape[1]
            width = width_of(span, 640)
            for c in range(0, span, width):
                total = None if start is None else refs[0][:, column + c : column + c + width]
                for x, y, row in pairs:
                    count = x_refs[x].shape[0]
                    part = dot_on(x_refs[x][...], y_refs[y][row : row + count, c : c + width], 0, 0)
                    total = part if total is None else total + part
                store(column + c, column + c + width, total)
            done.append((column, column + span))
        edge = 0
        for a, b in sorted(done) + [(n, n)]:
            if a > edge:
                rest = jnp.zeros((height, a - edge), F32) if start is None else refs[0][:, edge:a]
                store(edge, a, rest)
            edge = b

    x_spec = [pl.BlockSpec((x.shape[0], height), lambda i: (0, i)) for x in xs]
    more_spec = []
    if start is not None:
        more_spec.append(pl.BlockSpec((height, n), lambda i: (i, 0)))
    aliases = {}
    if place is None:
        shape, spec = (depth, n), pl.BlockSpec((height, n), lambda i: (i, 0))
    else:
        slot = place[0]
        shape, spec = (2, depth, n), pl.BlockSpec((1, height, n), lambda i: (slot, i, 0))
        if place[1] is not None:
            more_spec.append(ANY)
            aliases = {len(xs) + len(ys) + len(more) - 1: 0}
    return pl.pallas_call(
        kernel,
        grid=(depth // height,),
        in_specs=x_spec + [once(y.shape) for y in ys] + more_spec,
        out_specs=spec,
        out_shape=jax.ShapeDtypeStruct(shape, kind),
        input_output_aliases=aliases,
        compiler_params=pltpu.CompilerParams(vmem_limit_bytes=room << 20),
        cost_estimate=FREE,
        name="weight_terms",
    )(*xs, *ys, *more)


def across(x):
    length = lax.axis_size("dp")
    pairs = [(i, i - 1 + 2 * (i % 2)) for i in range(length)]
    return lax.ppermute(x, "dp", [(i, j) for i, j in pairs if 0 <= j < length])


def inside(x):
    return lax.ppermute(x, "dp", [(i, i ^ 1) for i in range(lax.axis_size("dp"))])


def over_dp(x, by, start=0, step=1):
    length = lax.axis_size("dp")
    pairs = [(i, i + by) for i in range(start, length, step) if 0 <= i + by < length]
    return lax.ppermute(x, "dp", pairs)


def near_rows(kv, swap):
    half = kv.shape[0] // 2

    def head(x):
        return lax.dynamic_slice_in_dim(x, swap * half, EDGE)

    def tail(x):
        return lax.dynamic_slice_in_dim(x, (1 - swap) * half, EDGE)

    left, right = over_dp(kv, 1), over_dp(kv, -1)
    far_left, far_right = over_dp(tail(kv), 2, 0, 2), over_dp(head(kv), -2, 1, 2)
    return (
        far_left,
        over_dp(tail(left), 1, 0, 2),
        left,
        kv,
        right,
        far_right,
        over_dp(head(right), -1, 1, 2),
    )


BLOCK = 256


def add_far(near, far, second):
    rows, width = far.shape
    steps = rows // BLOCK

    def kernel(second_ref, near_ref, far_ref, out_ref):
        out_ref[...] = (near_ref[...].astype(F32) + far_ref[...].astype(F32)).astype(BF)

    here = pl.BlockSpec((BLOCK, width), lambda i, s: (s[0] * steps + i, 0))
    return pl.pallas_call(
        kernel,
        grid_spec=pltpu.PrefetchScalarGridSpec(
            num_scalar_prefetch=1,
            grid=(steps,),
            in_specs=[here, pl.BlockSpec((BLOCK, width), lambda i, s: (i, 0))],
            out_specs=here,
        ),
        out_shape=jax.ShapeDtypeStruct(near.shape, BF),
        input_output_aliases={1: 0},
        cost_estimate=FREE,
        name="add_far",
    )(second[None], near, far)


def return_rows(grads, place):
    swap, core = place[0], place[1]
    near_inside, near_across, own, far_across, far_inside = grads
    head, tail = swap, 1 - swap
    near_across = add_far(near_across, inside(far_inside), jnp.where(core == 0, tail, head))
    from_across = across(near_across)
    near_inside = add_far(near_inside, across(far_across), jnp.where(core == 0, head, tail))
    return (own, from_across, inside(near_inside)), near_across


def add_returned(parts):
    rows, width = parts[0].shape

    def kernel(*refs):
        refs[-1][...] = sum(ref[...].astype(F32) for ref in refs[:-1]).astype(BF)

    block = pl.BlockSpec((BLOCK, width), lambda i: (i, 0))
    return pl.pallas_call(
        kernel,
        grid=(rows // BLOCK,),
        in_specs=[block] * len(parts),
        out_specs=block,
        out_shape=jax.ShapeDtypeStruct((rows, width), BF),
        cost_estimate=FREE,
        name="add_returned",
    )(*parts)


def sum_everywhere(x, axis):
    length = lax.axis_size(axis)
    bit = 1
    while bit < length:
        x = x + lax.ppermute(x, axis, [(i, i ^ bit) for i in range(length)])
        bit *= 2
    return x


class Order:
    def __init__(self):
        self.last = None

    def after(self, x, *more):
        if self.last is not None:
            more += (self.last,)
        return lax.optimization_barrier((x, *more))[0] if more else x

    def done(self, x):
        self.last = x
        return x


def partner(x):
    return lax.ppermute(x, "tensor", [(0, 1), (1, 0)])


def collect(x):
    if lax.axis_size("tensor") != 2:
        return [lax.all_gather(x, "tensor", axis=0, tiled=True)]
    return [x, partner(x)]


def share(parts):
    if len(parts) == 1:
        return lax.psum_scatter(parts[0], "tensor", scatter_dimension=0, tiled=True), jnp.zeros((), BF)
    return parts[0], partner(parts[1])


def norm_parts(x):
    centred = x - jnp.mean(x, axis=-1, keepdims=True)
    scale = lax.rsqrt(jnp.mean(centred * centred, axis=-1, keepdims=True) + EPSILON)
    return centred * scale, scale


def norm_back_rows(near, far, x, gain, base):
    rows, width = near.shape
    step = math.gcd(rows, 128)
    far = jnp.broadcast_to(far, near.shape)

    def kernel(near_ref, far_ref, x_ref, gain_ref, base_ref, out_ref, low_ref, sums_ref):
        grad = near_ref[...].astype(F32) + far_ref[...].astype(F32)
        z, scale = norm_parts(x_ref[...].astype(F32))
        e = grad * gain_ref[...]
        mean_e = jnp.mean(e, axis=-1, keepdims=True)
        mean_ez = jnp.mean(e * z, axis=-1, keepdims=True)
        before = base_ref[...].astype(F32)
        result = before + scale * (e - mean_e - z * mean_ez)
        out_ref[...] = result
        low_ref[...] = result.astype(BF)

        @pl.when(pl.program_id(0) == 0)
        def _():
            sums_ref[...] = jnp.zeros(sums_ref.shape, F32)

        for row, part in enumerate((grad * z, grad, result, before)):
            sums_ref[row : row + 1, :] += jnp.sum(part, axis=0, keepdims=True)

    block = pl.BlockSpec((step, width), lambda i: (i, 0))
    return pl.pallas_call(
        kernel,
        grid=(rows // step,),
        in_specs=[block, block, block, pl.BlockSpec((1, width), lambda i: (0, 0)), block],
        out_specs=(block, block, pl.BlockSpec((8, width), lambda i: (0, 0))),
        out_shape=(
            jax.ShapeDtypeStruct((rows, width), F32),
            jax.ShapeDtypeStruct((rows, width), BF),
            jax.ShapeDtypeStruct((8, width), F32),
        ),
        compiler_params=pltpu.CompilerParams(vmem_limit_bytes=26 << 20),
        cost_estimate=FREE,
        name="norm_back",
    )(near, far, x, gain[None, :], base)


def gelu_both(u):
    below = 0.5 * (1.0 + lax.erf(u * math.sqrt(0.5)))
    density = jnp.exp(-0.5 * u * u) * (1.0 / math.sqrt(2.0 * math.pi))
    return (u * below).astype(BF), (below + u * density).astype(BF)


def per_device(
    frames, cotangent, segment_ids, w_qkv, w_out, w_fc1, w_fc2, bias_qv, bias_fc1, norm_vectors
):
    dp_place = lax.axis_index("dp")
    paired = lax.axis_size("tensor") == 2
    swap = lax.axis_index("tensor").astype(jnp.int32) if paired else jnp.int32(0)
    own = frames.shape[1]
    FR = own * lax.axis_size("tensor")
    half = FR // 2
    rows = 2 * EDGE + 3 * FR
    local = w_qkv.shape[2]
    heads = local // HD
    W = -(-local // 128) * 128
    fill = W - local
    vectors = norm_vectors.astype(F32)

    def widened(x):
        return jnp.pad(x, [(0, 0)] * (x.ndim - 1) + [(0, fill)]) if fill else x

    attention = jnp.concatenate(
        (widened(w_qkv).reshape(w_qkv.shape[0], 3 * W), widened(w_out)), axis=1
    )
    att = lax.all_gather(attention[None], "dp", axis=1, tiled=True), 0
    bias_q = widened(bias_qv[0].astype(F32))
    bias_kv = jnp.concatenate((jnp.zeros((W,), F32), widened(bias_qv[1].astype(F32))))
    chosen = (jnp.arange(W)[:, None] // HD == jnp.arange(heads)[None, :]).astype(F32)
    order = Order()

    class Batch:
        pass

    batches = []
    for b in range(MB):
        m = Batch()
        batches.append(m)
        m.z1, m.r1 = norm_parts(frames[b].astype(F32))
        m.h1_own = (m.z1 * vectors[0] + vectors[1]).astype(BF)
        ids = segment_ids[b]
        reach = FR + EDGE
        padded = jnp.concatenate(
            (jnp.full((reach,), -1, jnp.int32), ids, jnp.full((reach,), 1 << 30, jnp.int32))
        )
        near = lax.dynamic_slice_in_dim(padded, dp_place * FR, rows)
        mine = jnp.concatenate(
            (
                lax.dynamic_slice_in_dim(ids, dp_place * FR + swap * half, half),
                lax.dynamic_slice_in_dim(ids, dp_place * FR + (1 - swap) * half, half),
            )
        )
        m.ranges = (
            jnp.sum((near[None, :] < mine[:, None]).astype(jnp.int32), axis=1),
            jnp.sum((near[None, :] <= mine[:, None]).astype(jnp.int32), axis=1),
        )
    m0, m1 = batches
    place = jnp.stack((swap, dp_place.astype(jnp.int32) % 2))
    for m in batches:
        m.h1 = collect(m.h1_own)

    def gated(xs, *wait):
        *rest, x = xs
        return [*rest, order.after(x, *wait)]

    def keys_values(m, *wait):
        m.kv = order.done(project_rows(gated(m.h1, *wait), att, W, 2 * W, bias_kv, 1.0, "keys_values"))

    def queries(m):
        m.q = order.done(project_rows(gated(m.h1), att, 0, W, bias_q, LOG2E * SCALE, "queries"))

    def attend(m, *wait):
        m.mixed, m.lse = attend_forward(order.after(m.q, *wait), m.pieces, m.ranges, place, heads)
        order.done(m.mixed)
        parts = back_rows([m.mixed], att, [3 * W], "attended")
        m.attended, m.attended_far = share(parts)
        order.done(parts[0])

    def second_norm(m):
        near, far = m.attended, order.after(m.attended_far)
        m.middle = frames[m.b].astype(F32) + near.astype(F32) + far.astype(F32) + vectors[4]
        m.z2, m.r2 = norm_parts(m.middle)
        h2 = order.done((m.z2 * vectors[2] + vectors[3]).astype(BF))
        m.h2 = collect(h2)

    def widen(m):
        m.active, m.slope = widen_rows(gated(m.h2), fc1, bias_fc1.astype(F32))
        order.done(m.slope)

    def grad_hidden(m):
        m.grad_u, m.grad_u_sum = slope_rows(gated(m.grad_f), fc2, m.slope)
        order.done(m.grad_u)

    def grad_normed(m):
        parts = back_rows(gated([m.grad_u]), fc1, [0], "grad_normed")
        m.grad_h2, m.grad_h2_far = share(parts)
        order.done(parts[0])

    def narrow(m, *wait):
        m.fed_parts = back_rows(gated([m.active], *wait), fc2, [0], "narrow")
        order.done(m.fed_parts[0])

    def send_narrow(m):
        *rest, last = m.fed_parts
        m.fed, m.fed_far = share([*rest, order.after(last)])

    def grad_second_norm(m):
        m.grad_middle, a, m.sums_two = norm_back_rows(
            m.grad_h2, order.after(m.grad_h2_far), m.middle, vectors[2], cotangent[m.b]
        )
        m.grad_a = collect(order.done(a))

    no_bias = jnp.zeros((W,), F32)

    def attend_back(m, *wait):
        m.grad_mixed = project_rows(
            gated(m.grad_a), att, 3 * W, W, no_bias, 1.0, "grad_mixed"
        )
        delta = lax.dot_general(
            chosen,
            m.grad_mixed.astype(F32) * m.mixed.astype(F32),
            (((0,), (1,)), ((), ())),
            precision=lax.Precision.HIGHEST,
        )
        m.grad_q, *grads = attend_backward(
            lax.optimization_barrier((m.q, *wait))[0] if wait else m.q, m.grad_mixed, m.pieces, m.ranges, m.lse, delta, place, heads
        )
        order.done(m.grad_q)
        m.grads = grads

    def send_back(m):
        near_inside, near_across, *rest = m.grads
        m.returned, m.ready = return_rows([near_inside, order.after(near_across), *rest], place)

    def add_up(m, *wait):
        m.grad_kv = order.done(add_returned([order.after(x, *wait) for x in m.returned]))

    def grad_projected(m):
        grad_kv = order.after(m.grad_kv)
        parts = back_rows([m.grad_q, grad_kv], att, [0, W], "grad_projected")
        m.grad_h1, m.grad_h1_far = share(parts)
        order.done(parts[0])

    def rows_of(xs, y):
        pairs, row = [], 0
        for x in xs:
            pairs.append((x, y, row))
            row += x.shape[0]
        return pairs

    def finish(m):
        m.inputs_grad, low, sums_one = norm_back_rows(
            m.grad_h1, order.after(m.grad_h1_far), frames[m.b], vectors[0], m.grad_middle
        )
        order.done(low)
        m.norm_sums = jnp.concatenate((sums_one[:2], m.sums_two[:4]))

    def owned(terms, axis):
        return lax.psum_scatter(terms.astype(BF), "dp", scatter_dimension=axis, tiled=True).astype(F32)

    m0.b, m1.b = 0, 1
    keys_values(m0, m1.h1[-1])
    keys_values(m1)
    queries(m0)
    queries(m1)
    m0.pieces = near_rows(m0.kv, swap)
    first_arrived = [m0.pieces[k] for k in (0, 2, 4, 5)]
    w_fc = lax.optimization_barrier((jnp.stack((w_fc1, w_fc2)), *first_arrived))[0]
    fc_all = lax.all_gather(w_fc, "dp", axis=1, tiled=True)
    fc1, fc2 = (fc_all, 0), (fc_all, 1)
    m1.pieces = near_rows(lax.optimization_barrier((m1.kv, m1.q, *first_arrived))[0], swap)
    for m in batches:
        m.grad_f = collect(lax.optimization_barrier((cotangent[m.b], m1.h1[-1]))[0])

    def term(x, y, *wait, **how):
        pairs = rows_of(gated(x, *wait), y)
        return order.done(weight_terms([(0, pairs)], w_fc1.shape[1], **how))

    attend(m0, m0.grad_f[-1], m1.grad_f[-1])
    second_norm(m0)
    attend(m1)
    widen(m0)
    grad_hidden(m0)
    grad_normed(m0)
    second_norm(m1)
    narrow(m0)
    fc2_term = term(m0.grad_f, m0.active, kind=F32)
    grad_second_norm(m0)
    fc1_term = term(m0.h2, m0.grad_u, kind=F32)
    widen(m1)
    grad_hidden(m1)
    grad_normed(m1)
    fc_terms = term(
        m1.grad_f, m1.active, m0.grad_a[-1], kind=BF, start=fc2_term, place=(1, None)
    )
    grad_second_norm(m1)
    fc_terms = term(m1.h2, m1.grad_u, kind=BF, start=fc1_term, place=(0, fc_terms))
    own_fc1, own_fc2 = owned(fc_terms, 1)
    attend_back(m0)
    send_back(m0)
    send_narrow(m0)
    attend_back(m1, m0.ready)
    narrow(m1, m0.fed_far)
    send_narrow(m1)
    terms = weight_terms(
        [
            (0, rows_of(gated(m0.h1), m0.grad_q) + rows_of(m1.h1, m1.grad_q)),
            (3 * W, rows_of(m0.grad_a, m0.mixed) + rows_of(m1.grad_a, m1.mixed)),
        ],
        4 * W,
        F32,
    )
    order.done(terms)
    send_back(m1)
    add_up(m0, m1.ready)
    grad_projected(m0)
    add_up(m1, m1.fed_far)
    kv_pairs = rows_of(m0.h1, m0.grad_kv) + rows_of(gated(m1.h1), m1.grad_kv)
    terms = order.done(weight_terms([(W, kv_pairs)], 4 * W, BF, start=terms, room=26))
    grad_projected(m1)
    own_attention = owned(lax.optimization_barrier((terms, own_fc1))[0], 0)
    finish(m0)
    outputs = [
        (m.middle + m.fed.astype(F32) + order.after(m.fed_far).astype(F32) + vectors[5]).astype(BF)
        for m in batches
    ]
    finish(m1)
    own_qkv = own_attention[:, : 3 * W].reshape(own_attention.shape[0], 3, W)[:, :, :local]
    own_out = own_attention[:, 3 * W :][:, :local]

    bias_parts = (
        sum(jnp.sum(m.grad_q, axis=0, dtype=F32) for m in batches)[:local],
        sum(jnp.sum(m.grad_kv[:, W:], axis=0, dtype=F32) for m in batches)[:local],
        sum(m.grad_u_sum[0] for m in batches),
    )
    norm_sums = m0.norm_sums + m1.norm_sums
    small = sum_everywhere(jnp.concatenate(bias_parts + (norm_sums.reshape(-1),)), "dp")
    bias_qv_total = small[: 2 * local].reshape(2, local)
    bias_fc1_total = small[2 * local : 2 * local + w_fc1.shape[1]]
    norm_total = sum_everywhere(small[2 * local + w_fc1.shape[1] :], "tensor").reshape(norm_sums.shape)
    return (
        jnp.stack(outputs),
        jnp.stack([m.inputs_grad for m in batches]),
        own_qkv,
        own_out,
        own_fc1,
        own_fc2,
        bias_qv_total,
        bias_fc1_total,
        norm_total,
    )


def solution(mesh):
    in_specs = (
        P(None, ("dp", "tensor"), None),
        P(None, ("dp", "tensor"), None),
        P(),
        P("dp", None, "tensor"),
        P("dp", "tensor"),
        P("dp", "tensor"),
        P("dp", "tensor"),
        P(None, "tensor"),
        P("tensor"),
        P(),
    )
    out_specs = (
        P(None, ("dp", "tensor"), None),
        P(None, ("dp", "tensor"), None),
        P("dp", None, "tensor"),
        P("dp", "tensor"),
        P("dp", "tensor"),
        P("dp", "tensor"),
        P(None, "tensor"),
        P("tensor"),
        P(),
    )
    return jax.shard_map(
        per_device, mesh=mesh, in_specs=in_specs, out_specs=out_specs, check_vma=False
    )
```
